128 devices in a mesh: dom: 16 (over y_lo, z, core), side: 4 (over x), rep: 2 (over y_hi).
Axes of the slice: x: 4, y: 4 (y_hi: 2, y_lo: 2; y = y_hi * 2 + y_lo), z: 4, core: 2. Of those that a mesh axis runs over, the one named last changes fastest.
Arguments:
- embeddings: bfloat16 [65536, 400], P('dom')
- relation: float32 [1345, 400], replicated, may hold values from 0.5 to 1.5
- source_ids: int32 [16, 4, 2, 8192], P('dom', 'side', 'rep'), may hold values from 0 to 4095
- relation_ids: int32 [16, 4, 2, 8192], P('dom', 'side', 'rep'), may hold values from 0 to 1344
- target_ids: int32 [16, 4, 2, 8192], P('dom', 'side', 'rep'), may hold values from 0 to 4095
- negative_ids: int32 [16, 4, 2, 8, 1000], P('dom', 'side', 'rep'), may hold values from 0 to 4095
- edge_counts: int32 [16, 4, 2], P('dom', 'side', 'rep'), may hold values from 1024 to 8192, as said below
- dirty: int32 [65536], P('dom'), may hold values 0 or 1
Outputs:
- updated: bfloat16 [65536, 400], P('dom')
- relation_grad: float32 [1345, 400], replicated
- checkpoint: bfloat16 [65536, 400], P('dom')
The draws below stay inside these ranges and needn't reach their ends.
Inputs may be any that keep to these rules, and one draw needn't show every extreme that they name: `edge_counts`: some list has exactly 8192 live slots in every draw.
All inputs are finite; a program needn't handle non-finite values. No bound on the sum of `dirty` on one device may be relied on, other than what follows from the above.
Results may differ from the reference program's by a relative error of at most 0.0077.
Values may be sent and summed in bfloat16 or wider, within the bound.
No kernel may reach another device: no remote copies, remote signals or barrier semaphores. Data moves between devices by JAX's collectives and lax.ppermute only.
A program may use at most 128 MiB of HBM per device.

```python
import jax
import jax.numpy as jnp
from jax import lax

D = 400
R = 1345
NEG = 1000
SPAN = 1024
ROWS = 4096
EDEV = 8192
BLOCKS = 8
NE = 65536
N_DOM = 16
N_SIDE = 4
N_REP = 2


def draw_embeddings(key, part):
    key = jax.random.fold_in(key, 3)
    base = 0.4 * jax.random.normal(key, (NE, D), jnp.float32)
    return jnp.clip(base, -2.4, 2.4).astype(jnp.bfloat16)


def draw_edge_counts(key, part):
    key = jax.random.fold_in(key, 5)
    counts = jax.random.randint(key, (N_DOM, N_SIDE, N_REP), EDEV // 8, EDEV + 1)
    return counts.at[0, 0, 0].set(EDEV).astype(jnp.int32)


def place_ends(result, rng, smallest, high):
    place = [jax.random.randint(jax.random.fold_in(rng, axis), (), 0, length) for axis, length in enumerate(result.shape)]
    longest = result.shape.index(max(result.shape))
    beside = place[:longest] + [(place[longest] + 1) % result.shape[longest]] + place[longest + 1:]
    return result.at[tuple(place)].set(smallest).at[tuple(beside)].set(high)


def setup_inputs(seed: int = 0) -> dict:
    key_list = jax.random.split(jax.random.key(seed), 9)
    return {
        "embeddings": draw_embeddings(jax.random.fold_in(key_list[8], 71), 0),
        "relation": jnp.clip(jax.random.uniform(key_list[1], (R, D), jnp.float32, 0.5, 1.5), 0.5, 1.5),
        "source_ids": place_ends(jax.random.randint(key_list[2], (N_DOM, N_SIDE, N_REP, EDEV), 0, ROWS), jax.random.fold_in(key_list[2], 1), 0, ROWS - 1).astype(jnp.int32),
        "relation_ids": place_ends(jax.random.randint(key_list[3], (N_DOM, N_SIDE, N_REP, EDEV), 0, R), jax.random.fold_in(key_list[3], 1), 0, R - 1).astype(jnp.int32),
        "target_ids": place_ends(jax.random.randint(key_list[4], (N_DOM, N_SIDE, N_REP, EDEV), 0, ROWS), jax.random.fold_in(key_list[4], 1), 0, ROWS - 1).astype(jnp.int32),
        "negative_ids": place_ends(jax.random.randint(key_list[5], (N_DOM, N_SIDE, N_REP, BLOCKS, NEG), 0, ROWS), jax.random.fold_in(key_list[5], 1), 0, ROWS - 1).astype(jnp.int32),
        "edge_counts": draw_edge_counts(jax.random.fold_in(key_list[8], 71), 0),
        "dirty": place_ends((jax.random.randint(key_list[7], (NE,), 0, 2) < 1).astype(jnp.int32), jax.random.fold_in(key_list[7], 1), 0, 1),
    }


def block_grads(slab, dst_slab, relation, src, rel_ids, dst, negs, live, acc):
    gsrc, gdst, grel = acc
    erows = slab[src]
    rrows = relation[rel_ids]
    left = (erows.astype(jnp.float32) * rrows).astype(jnp.bfloat16)
    drows = dst_slab[dst].astype(jnp.float32)
    nrows = dst_slab[negs]
    positive = jnp.sum(left.astype(jnp.float32) * drows, axis=1)
    negative = lax.dot_general(left, nrows, (((1,), (1,)), ((), ())), preferred_element_type=jnp.float32)
    top = jnp.maximum(positive, jnp.max(negative, axis=1))
    e_pos = jnp.exp(positive - top)
    e_neg = jnp.exp(negative - top[:, None])
    total = e_pos + jnp.sum(e_neg, axis=1)
    d_pos = live * (e_pos / total - 1.0)
    d_neg = (live[:, None] * e_neg / total[:, None]).astype(jnp.bfloat16)
    d_left = d_pos[:, None] * drows + jnp.dot(d_neg, nrows, preferred_element_type=jnp.float32)
    gsrc = gsrc.at[src].add(d_left * rrows)
    grel = grel.at[rel_ids].add(d_left * erows.astype(jnp.float32))
    gdst = gdst.at[dst].add(d_pos[:, None] * left.astype(jnp.float32))
    neg_part = lax.dot_general(d_neg, left, (((0,), (0,)), ((), ())), preferred_element_type=jnp.float32)
    gdst = gdst.at[negs].add(neg_part)
    return gsrc, gdst, grel


def reference(embeddings, relation, source_ids, relation_ids, target_ids, negative_ids, edge_counts, dirty):
    lists = N_SIDE * N_REP
    nblk = EDEV // SPAN

    def one_part(part):
        slab = lax.dynamic_slice_in_dim(embeddings, (part * ROWS).astype(jnp.int32), ROWS, 0)
        nxt = ((part + 1) % N_DOM).astype(jnp.int32)
        dst_slab = lax.dynamic_slice_in_dim(embeddings, nxt * ROWS, ROWS, 0)
        src = source_ids[part].reshape(lists * nblk, SPAN)
        rid = relation_ids[part].reshape(lists * nblk, SPAN)
        dst = target_ids[part].reshape(lists * nblk, SPAN)
        negs = negative_ids[part].reshape(lists * nblk, NEG)
        slots = jnp.arange(EDEV, dtype=jnp.int32)[None, :]
        live = (slots < edge_counts[part].reshape(lists, 1)).astype(jnp.float32).reshape(lists * nblk, SPAN)

        def step(acc, item):
            return block_grads(slab, dst_slab, relation, item[0], item[1], item[2], item[3], item[4], acc), None

        init = (jnp.zeros((ROWS, D), jnp.float32), jnp.zeros((ROWS, D), jnp.float32), jnp.zeros((R, D), jnp.float32))
        acc, _ = lax.scan(step, init, (src, rid, dst, negs, live))
        return acc

    gsrc, gdst, grel = lax.map(one_part, jnp.arange(N_DOM, dtype=jnp.int32))
    row_grad = gsrc + jnp.roll(gdst, 1, axis=0)
    updated = (embeddings.astype(jnp.float32) - 0.5 * row_grad.reshape(NE, D)).astype(jnp.bfloat16)
    checkpoint = jnp.where(dirty[:, None] == 1, updated, jnp.zeros_like(updated))
    return updated, jnp.sum(grel, axis=0), checkpoint
```

```python
import functools

import jax
import jax.numpy as jnp
from jax import lax
from jax.experimental import pallas as pl
from jax.experimental.pallas import tpu as pltpu
from jax.sharding import PartitionSpec as P

SPAN = 1024
LANES = 128
GROUPS = 4
REST = 16
FLAT = SPAN * GROUPS
CHUNK = 256
PIECES = 8
VMEM = 61 * 2**20

f32 = jnp.float32
bf16 = jnp.bfloat16


def shifted(x, axis, by):
    count = lax.axis_size(axis)
    return lax.ppermute(x, axis, [(i, (i + by) % count) for i in range(count)])


def row_of(index):
    return pl.ds(pl.multiple_of(index, GROUPS), GROUPS)


def slot_of(base, k):
    return pl.ds(base + (k // 8) * 8 * GROUPS + k % 8, GROUPS, stride=8)


def tiles(x):
    n = x.shape[0] // GROUPS
    x = x.reshape(n // 8, GROUPS, 8, LANES)
    return [x[:, c].reshape(n, LANES) for c in range(GROUPS)]


def untiles(cols):
    n = cols[0].shape[0]
    x = jnp.concatenate([c.reshape(n // 8, 1, 8, LANES) for c in cols], axis=1)
    return x.reshape(n * GROUPS, LANES)


def fill_rows(x, table, first, n):
    x = x.astype(f32)
    for c in range(GROUPS):
        part = x[:, c * LANES : min((c + 1) * LANES, x.shape[1])]
        if part.shape[1] < LANES:
            part = jnp.concatenate(
                [part, jnp.zeros((n, LANES - part.shape[1]), f32)], axis=1
            )
        table[pl.ds(first * GROUPS + c, n, stride=GROUPS), :] = part


def load_table(src_hbm, raw, sems, table):
    rows = src_hbm.shape[0]
    part = rows // 4
    copies = [
        pltpu.make_async_copy(
            src_hbm.at[pl.ds(i * part, part)], raw.at[pl.ds(i * part, part)], sems.at[i]
        )
        for i in range(4)
    ]
    for c in copies:
        c.start()
    for i in range(4):
        copies[i].wait()

        @pl.loop(0, part // 64)
        def _(q):
            first = pl.multiple_of(i * part + q * 64, 64)
            fill_rows(raw[pl.ds(first, 64), :], table, first, 64)


def edge_rows_kernel(count, src_i, rid_i, emb_hbm, rel_ref, e_out, r_out, ts, tr, raw, eb, rb, lsem, sems):
    load_table(emb_hbm, raw, lsem, ts)
    nrel = rel_ref.shape[0]
    whole = nrel // 64

    @pl.loop(0, whole)
    def _(q):
        first = pl.multiple_of(q * 64, 64)
        fill_rows(rel_ref[pl.ds(first, 64), :], tr, first, 64)

    for i in range(whole * 64, nrel):
        fill_rows(rel_ref[i : i + 1, :], tr, i, 1)

    nblocks = (count[0] + SPAN - 1) // SPAN

    def copies(blk, slot):
        return (
            pltpu.make_async_copy(eb.at[slot], e_out.at[blk], sems.at[slot, 0]),
            pltpu.make_async_copy(rb.at[slot], r_out.at[blk], sems.at[slot, 1]),
        )

    def step(blk, _):
        slot = lax.rem(blk, 2)

        @pl.when(blk >= 2)
        def _():
            for c in copies(blk - 2, slot):
                c.wait()

        es, rs = eb.at[slot], rb.at[slot]

        @pl.loop(0, SPAN // 16)
        def _(q):
            base = pl.multiple_of(q * 16 * GROUPS, 64)
            for k in range(16):
                j = blk * SPAN + q * 16 + k
                es[slot_of(base, k), :] = ts[row_of(src_i[j]), :]
                rs[slot_of(base, k), :] = tr[row_of(rid_i[j]), :]

        for c in copies(blk, slot):
            c.start()
        return 0

    lax.fori_loop(0, nblocks, step, 0)

    @pl.when(nblocks >= 2)
    def _():
        for c in copies(nblocks - 2, lax.rem(nblocks, 2)):
            c.wait()

    for c in copies(nblocks - 1, lax.rem(nblocks + 1, 2)):
        c.wait()


def write_piece(first, n, load, stage):
    for c in range(GROUPS - 1):
        stage[c * n : (c + 1) * n, :] = load(c, first, n).astype(stage.dtype)
    part = n // 8
    rest = load(GROUPS - 1, first, part)
    for k in range(1, 8):
        rest = rest + pltpu.roll(load(GROUPS - 1, first + k * part, part), k * REST, 1)
    stage[3 * n : 3 * n + part, :] = rest.astype(stage.dtype)


def block_kernel(
    nneg, count, src_i, rid_i, dst_i, neg_i, dst_hbm, e_hbm, r_hbm,
    gdst_out, gsrc_out, grel_out,
    td, asrc, adst, aneg, arel, raw, eb, rb, db, nb, lb, nbb, dn, stage, rstage, lsem, sems, osem,
):
    total = count[0]
    nblocks = (total + SPAN - 1) // SPAN

    def fetches(blk, slot):
        return (
            pltpu.make_async_copy(e_hbm.at[blk], eb.at[slot], sems.at[slot, 0]),
            pltpu.make_async_copy(r_hbm.at[blk], rb.at[slot], sems.at[slot, 1]),
        )

    for c in fetches(0, 0):
        c.start()
    load_table(dst_hbm, raw, lsem, td)
    for acc in (asrc, adst, aneg, arel):
        n = acc.shape[0] // 8

        @pl.loop(0, n // 16)
        def _(q):
            acc[pl.ds(pl.multiple_of(q * LANES, LANES), LANES), :] = jnp.zeros((LANES, LANES), f32)

        if n % 16:
            acc[(n // 16) * LANES :, :] = jnp.zeros((acc.shape[0] - (n // 16) * LANES, LANES), f32)

    def step(blk, _):
        slot = lax.rem(blk, 2)

        @pl.when(blk + 1 < nblocks)
        def _():
            for c in fetches(blk + 1, 1 - slot):
                c.start()

        first = blk * SPAN
        es, rs = eb.at[slot], rb.at[slot]

        @pl.loop(0, SPAN // 16)
        def _(q):
            base = pl.multiple_of(q * 16 * GROUPS, 64)
            for k in range(16):
                j = first + q * 16 + k
                db[slot_of(base, k), :] = td[row_of(dst_i[j]), :]
                nb[slot_of(base, k), :] = td[row_of(neg_i[j]), :]

        for ch in range(SPAN // CHUNK):
            cols = tiles(nb[ch * CHUNK * GROUPS : (ch + 1) * CHUNK * GROUPS, :])
            for c in range(GROUPS):
                nbb[ch * CHUNK : (ch + 1) * CHUNK, c * LANES : (c + 1) * LANES] = cols[c].astype(bf16)

        for c in fetches(blk, slot):
            c.wait()

        @pl.loop(0, SPAN // CHUNK)
        def _(ch):
            r0 = pl.multiple_of(ch * CHUNK, CHUNK)
            flat = pl.ds(pl.multiple_of(ch * CHUNK * GROUPS, CHUNK * GROUPS), CHUNK * GROUPS)
            e = tiles(es[flat, :])
            r = tiles(rs[flat, :])
            d = tiles(db[flat, :])
            left = [(e[c] * r[c]).astype(bf16) for c in range(GROUPS)]
            leftf = [x.astype(f32) for x in left]
            prod = leftf[0] * d[0]
            for c in range(1, GROUPS):
                prod = prod + leftf[c] * d[c]
            positive = jnp.sum(prod, axis=1, keepdims=True)
            lc = jnp.concatenate(left, axis=1)
            lb[pl.ds(r0, CHUNK), :] = lc
            negative = lax.dot_general(
                lc, nbb[...], (((1,), (1,)), ((), ())), preferred_element_type=f32
            )
            lane = lax.broadcasted_iota(jnp.int32, negative.shape, 1)
            negative = jnp.where(lane < nneg, negative, -jnp.inf)
            top = jnp.maximum(positive, jnp.max(negative, axis=1, keepdims=True))
            e_pos = jnp.exp(positive - top)
            e_neg = jnp.exp(negative - top)
            z = e_pos + jnp.sum(e_neg, axis=1, keepdims=True)
            row = lax.broadcasted_iota(jnp.int32, (CHUNK, 1), 0) + (first + r0)
            live = jnp.where(row < total, 1.0, 0.0).astype(f32)
            inv = 1.0 / z
            d_pos = live * (e_pos * inv - 1.0)
            d_neg = (e_neg * (live * inv)).astype(bf16)
            dn[pl.ds(r0, CHUNK), :] = d_neg
            dl = jnp.dot(d_neg, nbb[...], preferred_element_type=f32)
            x = [d_pos * d[c] + dl[:, c * LANES : (c + 1) * LANES] for c in range(GROUPS)]
            db[flat, :] = untiles([d_pos * leftf[c] for c in range(GROUPS)])
            es[flat, :] = untiles([x[c] * e[c] for c in range(GROUPS)])
            rs[flat, :] = untiles([x[c] * r[c] for c in range(GROUPS)])

        for ch in range(SPAN // CHUNK):
            part = lax.dot_general(
                dn[:, ch * CHUNK : (ch + 1) * CHUNK], lb[...], (((0,), (0,)), ((), ())),
                preferred_element_type=f32,
            )
            nb[ch * CHUNK * GROUPS : (ch + 1) * CHUNK * GROUPS, :] = untiles(
                [part[:, c * LANES : (c + 1) * LANES] for c in range(GROUPS)]
            )

        @pl.loop(0, SPAN // 16)
        def _(q):
            base = pl.multiple_of(q * 16 * GROUPS, 64)
            for k in range(16):
                j = first + q * 16 + k
                at = slot_of(base, k)
                for acc, idx, val in ((asrc, src_i, rs), (adst, dst_i, db), (aneg, neg_i, nb), (arel, rid_i, es)):
                    row = row_of(idx[j])
                    acc[row, :] = acc[row, :] + val[at, :]

        return 0

    lax.fori_loop(0, nblocks, step, 0)

    def emit(load, out, npieces, n, st):
        def copy(j, slot):
            return pltpu.make_async_copy(st.at[slot], out.at[j], osem.at[slot])

        @pl.loop(0, npieces)
        def _(j):
            slot = lax.rem(j, 2)

            @pl.when(j >= 2)
            def _():
                copy(j - 2, slot).wait()

            write_piece(j * n, n, load, st.at[slot])
            copy(j, slot).start()

        for j in (npieces - 2, npieces - 1):
            copy(j, j % 2).wait()

    def rows(acc):
        return lambda c, first, n: acc[pl.ds(first * GROUPS + c, n, stride=GROUPS), :]

    n = asrc.shape[0] // GROUPS // PIECES
    emit(lambda c, f, m: rows(adst)(c, f, m) + rows(aneg)(c, f, m), gdst_out, PIECES, n, stage)
    emit(rows(asrc), gsrc_out, PIECES, n, stage)
    emit(rows(arel), grel_out, grel_out.shape[0], LANES, rstage)


def smem():
    return pl.BlockSpec(memory_space=pltpu.SMEM)


def hbm():
    return pl.BlockSpec(memory_space=pl.ANY)


def edge_rows(count, src, rid, emb, relation):
    nb = src.shape[0] // SPAN
    rows = emb.shape[0]
    nrel = relation.shape[0]
    shape = jax.ShapeDtypeStruct((nb, FLAT, LANES), f32)
    return pl.pallas_call(
        edge_rows_kernel,
        out_shape=(shape, shape),
        in_specs=[smem()] * 3 + [hbm(), pl.BlockSpec(memory_space=pltpu.VMEM)],
        out_specs=(hbm(), hbm()),
        scratch_shapes=[
            pltpu.VMEM((rows * GROUPS, LANES), f32),
            pltpu.VMEM((-(-nrel // 8) * 8 * GROUPS, LANES), f32),
            pltpu.VMEM(emb.shape, bf16),
            pltpu.VMEM((2, FLAT, LANES), f32),
            pltpu.VMEM((2, FLAT, LANES), f32),
            pltpu.SemaphoreType.DMA((4,)),
            pltpu.SemaphoreType.DMA((2, 2)),
        ],
        compiler_params=pltpu.CompilerParams(vmem_limit_bytes=VMEM),
        cost_estimate=pl.CostEstimate(flops=0, bytes_accessed=60_000_000, transcendentals=0),
        name="edge_rows",
    )(count, src, rid, emb, relation)


def edge_blocks(nneg, count, src, rid, dst, neg, dst_slab, e_rows, r_rows, nrel):
    rows = dst_slab.shape[0]
    packed = rows // PIECES * 25 // 8
    relp = -(-nrel // LANES)
    arel = relp * LANES * GROUPS
    grad = jax.ShapeDtypeStruct((PIECES, packed, LANES), bf16)
    return pl.pallas_call(
        functools.partial(block_kernel, nneg),
        out_shape=(grad, grad, jax.ShapeDtypeStruct((relp, LANES * 25 // 8, LANES), f32)),
        in_specs=[smem()] * 5 + [hbm()] * 3,
        out_specs=(hbm(), hbm(), hbm()),
        scratch_shapes=[
            pltpu.VMEM((rows * GROUPS, LANES), f32),
            pltpu.VMEM((rows * GROUPS, LANES), f32),
            pltpu.VMEM((rows * GROUPS, LANES), f32),
            pltpu.VMEM((rows * GROUPS, LANES), f32),
            pltpu.VMEM((arel, LANES), f32),
            pltpu.VMEM(dst_slab.shape, bf16),
            pltpu.VMEM((2, FLAT, LANES), f32),
            pltpu.VMEM((2, FLAT, LANES), f32),
            pltpu.VMEM((FLAT, LANES), f32),
            pltpu.VMEM((FLAT, LANES), f32),
            pltpu.VMEM((SPAN, LANES * GROUPS), bf16),
            pltpu.VMEM((SPAN, LANES * GROUPS), bf16),
            pltpu.VMEM((SPAN, SPAN), bf16),
            pltpu.VMEM((2, packed, LANES), bf16),
            pltpu.VMEM((2, LANES * 25 // 8, LANES), f32),
            pltpu.SemaphoreType.DMA((4,)),
            pltpu.SemaphoreType.DMA((2, 2)),
            pltpu.SemaphoreType.DMA((2,)),
        ],
        compiler_params=pltpu.CompilerParams(vmem_limit_bytes=VMEM),
        name="edge_blocks",
    )(count, src, rid, dst, neg, dst_slab, e_rows, r_rows)


def unpack(x, n):
    part = n // 8
    rest = x[3 * n :]
    cols = jnp.concatenate(
        [rest if k == 0 else pltpu.roll(rest, LANES - k * REST, 1) for k in range(8)], axis=0
    )
    return jnp.concatenate([x[:n], x[n : 2 * n], x[2 * n : 3 * n], cols[:, :REST]], axis=1)


def update_kernel(a_ref, b_ref, emb_ref, out_ref):
    n = emb_ref.shape[0]
    part = n // 8
    g = jnp.sum(a_ref[...].astype(f32), axis=0) + jnp.sum(b_ref[...].astype(f32), axis=0)
    e = emb_ref[...].astype(f32)
    for c in range(GROUPS - 1):
        out_ref[c * n : (c + 1) * n, :] = (
            e[:, c * LANES : (c + 1) * LANES] - 0.5 * g[c * n : (c + 1) * n]
        ).astype(bf16)
    rest = -0.5 * g[3 * n :]
    last = jnp.concatenate([e[:, 3 * LANES :], jnp.zeros((n, LANES - REST), f32)], axis=1)
    for k in range(8):
        x = last[k * part : (k + 1) * part]
        rest = rest + (x if k == 0 else pltpu.roll(x, k * REST, 1))
    out_ref[3 * n :, :] = rest.astype(bf16)


def update(a, b, emb):
    n = emb.shape[0]
    return pl.pallas_call(
        update_kernel,
        out_shape=jax.ShapeDtypeStruct((n * 25 // 8, LANES), bf16),
        compiler_params=pltpu.CompilerParams(vmem_limit_bytes=VMEM),
        name="update",
    )(a, b, emb)


def finish_kernel(x_ref, dirty_ref, up_ref, check_ref):
    n = up_ref.shape[0]
    rows = unpack(x_ref[0].astype(f32), n)
    up_ref[...] = rows.astype(bf16)
    check_ref[...] = jnp.where(dirty_ref[...] == 1, rows, 0.0).astype(bf16)


def finish(x, dirty, width):
    pieces, packed, _ = x.shape
    n = packed * 8 // 25
    out = jax.ShapeDtypeStruct((pieces * n, width), bf16)
    return pl.pallas_call(
        finish_kernel,
        grid=(pieces,),
        in_specs=[
            pl.BlockSpec((1, packed, LANES), lambda i: (i, 0, 0)),
            pl.BlockSpec((n, 1), lambda i: (i, 0)),
        ],
        out_specs=[pl.BlockSpec((n, width), lambda i: (i, 0))] * 2,
        out_shape=(out, out),
        compiler_params=pltpu.CompilerParams(vmem_limit_bytes=VMEM),
        name="finish",
    )(x, dirty)


def relation_kernel(x_ref, out_ref):
    for i in range(x_ref.shape[0]):
        rows = unpack(x_ref[i], LANES)
        n = min(LANES, out_ref.shape[0] - i * LANES)
        out_ref[i * LANES : i * LANES + n, :] = rows[:n]


def relation_out(x, shape):
    return pl.pallas_call(
        relation_kernel,
        out_shape=jax.ShapeDtypeStruct(shape, f32),
        compiler_params=pltpu.CompilerParams(vmem_limit_bytes=VMEM),
        name="relation_out",
    )(x)


def local(
    embeddings, relation, source_ids, relation_ids, target_ids, negative_ids, edge_counts, dirty
):
    rows, width = embeddings.shape
    count = edge_counts.reshape(1)
    nneg = negative_ids.shape[-1]
    src = source_ids.reshape(-1) * GROUPS
    rid = relation_ids.reshape(-1) * GROUPS
    dst = target_ids.reshape(-1) * GROUPS
    neg = (jnp.pad(negative_ids[0, 0, 0], ((0, 0), (0, SPAN - nneg))) * GROUPS).reshape(-1)

    dst_slab = shifted(embeddings, "dom", -1)
    e_rows, r_rows = edge_rows(count, src, rid, embeddings, relation)
    gdst, gsrc, grel = edge_blocks(
        nneg, count, src, rid, dst, neg, dst_slab, e_rows, r_rows, relation.shape[0]
    )

    returned = shifted(gdst, "dom", 1)
    a = lax.all_to_all(gsrc, ("side", "rep"), 0, 0, tiled=True)
    b = lax.all_to_all(returned, ("side", "rep"), 0, 0, tiled=True)
    me = lax.axis_index("side") * lax.axis_size("rep") + lax.axis_index("rep")
    piece = rows // PIECES
    own = lax.dynamic_slice_in_dim(embeddings, me * piece, piece, 0)
    mine = update(a, b, own)
    both = lax.all_gather(mine, "rep")
    gathered = lax.all_gather(both, "side").reshape(PIECES, -1, LANES)
    updated, checkpoint = finish(gathered, dirty[:, None], width)
    relation_grad = relation_out(lax.psum(grel, ("dom", "side", "rep")), relation.shape)
    return (updated, relation_grad, checkpoint)


def solution(mesh):
    placed = (
        P("dom", None),
        P(),
        P("dom", "side", "rep", None),
        P("dom", "side", "rep", None),
        P("dom", "side", "rep", None),
        P("dom", "side", "rep", None, None),
        P("dom", "side", "rep"),
        P("dom"),
    )
    return jax.shard_map(
        local,
        mesh=mesh,
        in_specs=placed,
        out_specs=(P("dom", None), P(), P("dom", None)),
        check_vma=False,
    )
```

```python
import functools

import jax
import jax.numpy as jnp
from jax import lax
from jax.experimental import pallas as pl
from jax.experimental.pallas import tpu as pltpu
from jax.sharding import PartitionSpec as P

SPAN = 1024
LANES = 128
GROUPS = 4
REST = 16
FLAT = SPAN * GROUPS
CHUNK = 256
PIECES = 8
VMEM = 61 * 2**20

f32 = jnp.float32
bf16 = jnp.bfloat16


def shifted(x, axis, by):
    count = lax.axis_size(axis)
    return lax.ppermute(x, axis, [(i, (i + by) % count) for i in range(count)])


def row_of(index):
    return pl.ds(pl.multiple_of(index, GROUPS), GROUPS)


def slot_of(base, k):
    return pl.ds(base + (k // 8) * 8 * GROUPS + k % 8, GROUPS, stride=8)


def tiles(x):
    n = x.shape[0] // GROUPS
    x = x.reshape(n // 8, GROUPS, 8, LANES)
    return [x[:, c].reshape(n, LANES) for c in range(GROUPS)]


def untiles(cols):
    n = cols[0].shape[0]
    x = jnp.concatenate([c.reshape(n // 8, 1, 8, LANES) for c in cols], axis=1)
    return x.reshape(n * GROUPS, LANES)


def fill_rows(x, table, first, n):
    x = x.astype(f32)
    for c in range(GROUPS):
        part = x[:, c * LANES : min((c + 1) * LANES, x.shape[1])]
        if part.shape[1] < LANES:
            part = jnp.concatenate(
                [part, jnp.zeros((n, LANES - part.shape[1]), f32)], axis=1
            )
        table[pl.ds(first * GROUPS + c, n, stride=GROUPS), :] = part


def load_table(src_hbm, raw, sems, table):
    part = raw.shape[1]
    count = src_hbm.shape[0] // part

    def copy(i, slot):
        return pltpu.make_async_copy(
            src_hbm.at[pl.ds(pl.multiple_of(i * part, part), part)], raw.at[slot], sems.at[slot]
        )

    for i in range(2):
        copy(i, i).start()

    @pl.loop(0, count)
    def _(i):
        slot = lax.rem(i, 2)
        copy(i, slot).wait()

        @pl.loop(0, part // 64)
        def _(q):
            at = pl.multiple_of(q * 64, 64)
            fill_rows(raw[slot, pl.ds(at, 64), :], table, i * part + at, 64)

        @pl.when(i + 2 < count)
        def _():
            copy(i + 2, slot).start()


def edge_rows_kernel(count, src_i, rid_i, emb_hbm, rel_ref, e_out, r_out, ts, tr, raw, eb, rb, lsem, sems):
    load_table(emb_hbm, raw, lsem, ts)
    nrel = rel_ref.shape[0]
    whole = nrel // 64

    @pl.loop(0, whole)
    def _(q):
        first = pl.multiple_of(q * 64, 64)
        fill_rows(rel_ref[pl.ds(first, 64), :], tr, first, 64)

    for i in range(whole * 64, nrel):
        fill_rows(rel_ref[i : i + 1, :], tr, i, 1)

    nblocks = (count[0] + SPAN - 1) // SPAN

    def copies(blk, slot):
        return (
            pltpu.make_async_copy(eb.at[slot], e_out.at[blk], sems.at[slot, 0]),
            pltpu.make_async_copy(rb.at[slot], r_out.at[blk], sems.at[slot, 1]),
        )

    def step(blk, _):
        slot = lax.rem(blk, 2)

        @pl.when(blk >= 2)
        def _():
            for c in copies(blk - 2, slot):
                c.wait()

        es, rs = eb.at[slot], rb.at[slot]

        @pl.loop(0, SPAN // 16)
        def _(q):
            base = pl.multiple_of(q * 16 * GROUPS, 64)
            for k in range(16):
                j = blk * SPAN + q * 16 + k
                es[slot_of(base, k), :] = ts[row_of(src_i[j]), :]
                rs[slot_of(base, k), :] = tr[row_of(rid_i[j]), :]

        for c in copies(blk, slot):
            c.start()
        return 0

    lax.fori_loop(0, nblocks, step, 0)

    @pl.when(nblocks >= 2)
    def _():
        for c in copies(nblocks - 2, lax.rem(nblocks, 2)):
            c.wait()

    for c in copies(nblocks - 1, lax.rem(nblocks + 1, 2)):
        c.wait()


def write_piece(first, n, load, stage):
    for c in range(GROUPS - 1):
        stage[c * n : (c + 1) * n, :] = load(c, first, n).astype(stage.dtype)
    part = n // 8
    rest = load(GROUPS - 1, first, part)
    for k in range(1, 8):
        rest = rest + pltpu.roll(load(GROUPS - 1, first + k * part, part), k * REST, 1)
    stage[3 * n : 3 * n + part, :] = rest.astype(stage.dtype)


def zero(acc):
    n = acc.shape[0]
    whole = n // 256

    @pl.loop(0, whole)
    def _(q):
        acc[pl.ds(pl.multiple_of(q * 256, 256), 256), :] = jnp.zeros((256, LANES), f32)

    if n % 256:
        acc[whole * 256 :, :] = jnp.zeros((n - whole * 256, LANES), f32)


def add_rows(ops):
    values = [val[at, :] for _, _, val, at in ops]
    held = [acc[row, :] for acc, row, _, _ in ops]
    for (acc, row, _, _), v, h in zip(ops, values, held):
        acc[row, :] = h + v


def plane(accs):
    def load(c, first, n):
        at = pl.ds(first * GROUPS + c, n, stride=GROUPS)
        x = accs[0][at, :]
        for acc in accs[1:]:
            x = x + acc[at, :]
        return x

    return load


def block_kernel(
    nneg, count, rid_i, dst_i, neg_i, dst_hbm, e_hbm, r_hbm,
    grad_out, v_out,
    td, a0, a1, a2, r0_acc, r1_acc, raw, eb, rb, db, nb, lb, nbb, dn, stage, lsem, sems, vsem, osem,
):
    total = count[0]
    nblocks = (total + SPAN - 1) // SPAN

    def fetches(blk, slot):
        return (
            pltpu.make_async_copy(e_hbm.at[blk], eb.at[slot], sems.at[slot, 0]),
            pltpu.make_async_copy(r_hbm.at[blk], rb.at[slot], sems.at[slot, 1]),
        )

    def put(blk, slot):
        return pltpu.make_async_copy(rb.at[slot], v_out.at[blk], vsem.at[slot])

    for c in fetches(0, 0):
        c.start()
    load_table(dst_hbm, raw, lsem, td)
    for acc in (a0, a1, a2, r0_acc, r1_acc):
        zero(acc)

    def step(blk, _):
        slot = lax.rem(blk, 2)

        @pl.when(blk >= 1)
        def _():
            put(blk - 1, 1 - slot).wait()

        @pl.when(blk + 1 < nblocks)
        def _():
            for c in fetches(blk + 1, 1 - slot):
                c.start()

        first = blk * SPAN
        es, rs = eb.at[slot], rb.at[slot]

        @pl.loop(0, SPAN // 16)
        def _(q):
            base = pl.multiple_of(q * 16 * GROUPS, 64)
            for k in range(16):
                j = first + q * 16 + k
                db[slot_of(base, k), :] = td[row_of(dst_i[j]), :]
                nb[slot_of(base, k), :] = td[row_of(neg_i[j]), :]

        for ch in range(SPAN // CHUNK):
            cols = tiles(nb[ch * CHUNK * GROUPS : (ch + 1) * CHUNK * GROUPS, :])
            for c in range(GROUPS):
                nbb[ch * CHUNK : (ch + 1) * CHUNK, c * LANES : (c + 1) * LANES] = cols[c].astype(bf16)

        for c in fetches(blk, slot):
            c.wait()

        @pl.loop(0, SPAN // CHUNK)
        def _(ch):
            r0 = pl.multiple_of(ch * CHUNK, CHUNK)
            flat = pl.ds(pl.multiple_of(ch * CHUNK * GROUPS, CHUNK * GROUPS), CHUNK * GROUPS)
            e = tiles(es[flat, :])
            r = tiles(rs[flat, :])
            d = tiles(db[flat, :])
            left = [(e[c] * r[c]).astype(bf16) for c in range(GROUPS)]
            leftf = [x.astype(f32) for x in left]
            prod = leftf[0] * d[0]
            for c in range(1, GROUPS):
                prod = prod + leftf[c] * d[c]
            positive = jnp.sum(prod, axis=1, keepdims=True)
            lc = jnp.concatenate(left, axis=1)
            lb[pl.ds(r0, CHUNK), :] = lc
            negative = lax.dot_general(
                lc, nbb[...], (((1,), (1,)), ((), ())), preferred_element_type=f32
            )
            lane = lax.broadcasted_iota(jnp.int32, negative.shape, 1)
            negative = jnp.where(lane < nneg, negative, -jnp.inf)
            top = jnp.maximum(positive, jnp.max(negative, axis=1, keepdims=True))
            e_pos = jnp.exp(positive - top)
            e_neg = jnp.exp(negative - top)
            z = e_pos + jnp.sum(e_neg, axis=1, keepdims=True)
            row = lax.broadcasted_iota(jnp.int32, (CHUNK, 1), 0) + (first + r0)
            live = jnp.where(row < total, 1.0, 0.0).astype(f32)
            inv = 1.0 / z
            d_pos = live * (e_pos * inv - 1.0)
            d_neg = (e_neg * (live * inv)).astype(bf16)
            dn[pl.ds(r0, CHUNK), :] = d_neg
            dl = jnp.dot(d_neg, nbb[...], preferred_element_type=f32)
            x = [d_pos * d[c] + dl[:, c * LANES : (c + 1) * LANES] for c in range(GROUPS)]
            db[flat, :] = untiles([d_pos * leftf[c] for c in range(GROUPS)])
            es[flat, :] = untiles([x[c] * e[c] for c in range(GROUPS)])
            rs[flat, :] = untiles([x[c] * r[c] for c in range(GROUPS)])

        put(blk, slot).start()

        for ch in range(SPAN // CHUNK):
            part = lax.dot_general(
                dn[:, ch * CHUNK : (ch + 1) * CHUNK], lb[...], (((0,), (0,)), ((), ())),
                preferred_element_type=f32,
            )
            nb[ch * CHUNK * GROUPS : (ch + 1) * CHUNK * GROUPS, :] = untiles(
                [part[:, c * LANES : (c + 1) * LANES] for c in range(GROUPS)]
            )

        def scatter(j0, base, n):
            for t in range(0, n, 3):
                ks = list(range(t, min(t + 3, n)))
                at = [slot_of(base, k) for k in ks]
                copies = (a0, a1, a2)
                dst = [(copies[i], row_of(dst_i[j0 + k]), db, at[i]) for i, k in enumerate(ks)]
                neg = [(copies[i], row_of(neg_i[j0 + k]), nb, at[i]) for i, k in enumerate(ks)]
                rel = [
                    ((r0_acc, r1_acc)[i % 2], row_of(rid_i[j0 + k]), es, at[i])
                    for i, k in enumerate(ks)
                ]
                add_rows(dst + rel[:2])
                add_rows(neg + rel[2:])

        @pl.loop(0, SPAN // 24)
        def _(q):
            scatter(first + q * 24, pl.multiple_of(q * 24 * GROUPS, 32), 24)

        done = SPAN // 24 * 24
        scatter(first + done, done * GROUPS, SPAN - done)
        return 0

    lax.fori_loop(0, nblocks, step, 0)
    last = nblocks - 1
    put(last, lax.rem(last, 2)).wait()

    n = td.shape[0] // GROUPS // PIECES
    m = r0_acc.shape[0] // GROUPS // PIECES
    packed = n * 25 // 8
    relp = m * 25 // 8
    pad = grad_out.shape[1] - packed - relp
    grad, rel = plane((a0, a1, a2)), plane((r0_acc, r1_acc))

    def fill(j, st):
        write_piece(j * n, n, grad, st)
        write_piece(j * m, m, rel, st.at[pl.ds(packed, relp)])
        if pad:
            st[packed + relp :, :] = jnp.zeros((pad, LANES), st.dtype)

    emit(fill, grad_out, stage, osem)


def emit(fill, out, stage, sem):
    def copy(j, slot):
        return pltpu.make_async_copy(stage.at[slot], out.at[j], sem.at[slot])

    @pl.loop(0, PIECES)
    def _(j):
        slot = lax.rem(j, 2)

        @pl.when(j >= 2)
        def _():
            copy(j - 2, slot).wait()

        fill(j, stage.at[slot])
        copy(j, slot).start()

    for j in (PIECES - 2, PIECES - 1):
        copy(j, j % 2).wait()


def source_kernel(count, src_i, v_hbm, grad_out, a0, a1, a2, a3, vb, stage, sems, osem):
    nblocks = (count[0] + SPAN - 1) // SPAN
    accs = (a0, a1, a2, a3)

    def fetch(blk, slot):
        return pltpu.make_async_copy(v_hbm.at[blk], vb.at[slot], sems.at[slot])

    fetch(0, 0).start()
    for acc in accs:
        zero(acc)

    def step(blk, _):
        slot = lax.rem(blk, 2)

        @pl.when(blk + 1 < nblocks)
        def _():
            fetch(blk + 1, 1 - slot).start()

        fetch(blk, slot).wait()
        vs = vb.at[slot]

        @pl.loop(0, SPAN // 16)
        def _(q):
            base = pl.multiple_of(q * 16 * GROUPS, 64)
            for t in range(0, 16, 4):
                add_rows(
                    [
                        (accs[i], row_of(src_i[blk * SPAN + q * 16 + t + i]), vs, slot_of(base, t + i))
                        for i in range(4)
                    ]
                )

        return 0

    lax.fori_loop(0, nblocks, step, 0)
    n = a0.shape[0] // GROUPS // PIECES
    load = plane(accs)
    emit(lambda j, st: write_piece(j * n, n, load, st), grad_out, stage, osem)


def smem():
    return pl.BlockSpec(memory_space=pltpu.SMEM)


def hbm():
    return pl.BlockSpec(memory_space=pl.ANY)


def edge_rows(count, src, rid, emb, relation):
    nb = src.shape[0] // SPAN
    rows = emb.shape[0]
    nrel = relation.shape[0]
    shape = jax.ShapeDtypeStruct((nb, FLAT, LANES), f32)
    return pl.pallas_call(
        edge_rows_kernel,
        out_shape=(shape, shape),
        in_specs=[smem()] * 3 + [hbm(), pl.BlockSpec(memory_space=pltpu.VMEM)],
        out_specs=(hbm(), hbm()),
        scratch_shapes=[
            pltpu.VMEM((rows * GROUPS, LANES), f32),
            pltpu.VMEM((-(-nrel // 8) * 8 * GROUPS, LANES), f32),
            pltpu.VMEM((2, 512, emb.shape[1]), bf16),
            pltpu.VMEM((2, FLAT, LANES), f32),
            pltpu.VMEM((2, FLAT, LANES), f32),
            pltpu.SemaphoreType.DMA((2,)),
            pltpu.SemaphoreType.DMA((2, 2)),
        ],
        compiler_params=pltpu.CompilerParams(vmem_limit_bytes=VMEM),
        cost_estimate=pl.CostEstimate(flops=0, bytes_accessed=60_000_000, transcendentals=0),
        name="edge_rows",
    )(count, src, rid, emb, relation)


def edge_blocks(nneg, count, rid, dst, neg, dst_slab, e_rows, r_rows, nrel):
    rows = dst_slab.shape[0]
    packed = rows // PIECES * 25 // 8
    relm = -(-nrel // (PIECES * 64)) * 64
    wire = -(-(packed + relm * 25 // 8) // 16) * 16
    table = pltpu.VMEM((rows * GROUPS, LANES), f32)
    rel = pltpu.VMEM((relm * PIECES * GROUPS, LANES), f32)
    return pl.pallas_call(
        functools.partial(block_kernel, nneg),
        out_shape=(
            jax.ShapeDtypeStruct((PIECES, wire, LANES), bf16),
            jax.ShapeDtypeStruct(r_rows.shape, f32),
        ),
        in_specs=[smem()] * 4 + [hbm()] * 3,
        out_specs=(hbm(), hbm()),
        scratch_shapes=[
            table, table, table, table, rel, rel,
            pltpu.VMEM((2, 512, dst_slab.shape[1]), bf16),
            pltpu.VMEM((2, FLAT, LANES), f32),
            pltpu.VMEM((2, FLAT, LANES), f32),
            pltpu.VMEM((FLAT, LANES), f32),
            pltpu.VMEM((FLAT, LANES), f32),
            pltpu.VMEM((SPAN, LANES * GROUPS), bf16),
            pltpu.VMEM((SPAN, LANES * GROUPS), bf16),
            pltpu.VMEM((SPAN, SPAN), bf16),
            pltpu.VMEM((2, wire, LANES), bf16),
            pltpu.SemaphoreType.DMA((2,)),
            pltpu.SemaphoreType.DMA((2, 2)),
            pltpu.SemaphoreType.DMA((2,)),
            pltpu.SemaphoreType.DMA((2,)),
        ],
        compiler_params=pltpu.CompilerParams(vmem_limit_bytes=VMEM),
        name="edge_blocks",
    )(count, rid, dst, neg, dst_slab, e_rows, r_rows)


def source_rows(count, src, values, rows):
    packed = rows // PIECES * 25 // 8
    table = pltpu.VMEM((rows * GROUPS, LANES), f32)
    return pl.pallas_call(
        source_kernel,
        out_shape=jax.ShapeDtypeStruct((PIECES, packed, LANES), bf16),
        in_specs=[smem()] * 2 + [hbm()],
        out_specs=hbm(),
        scratch_shapes=[
            table, table, table, table,
            pltpu.VMEM((2, FLAT, LANES), f32),
            pltpu.VMEM((2, packed, LANES), bf16),
            pltpu.SemaphoreType.DMA((2,)),
            pltpu.SemaphoreType.DMA((2,)),
        ],
        compiler_params=pltpu.CompilerParams(vmem_limit_bytes=VMEM),
        cost_estimate=pl.CostEstimate(flops=0, bytes_accessed=60_000_000, transcendentals=0),
        name="source_rows",
    )(count, src, values)


def sum_kernel(x_ref, rows_ref, rel_ref):
    n = rows_ref.shape[0]
    m = x_ref.shape[1] - n
    total = jnp.sum(x_ref[...].astype(f32), axis=0)
    rows_ref[...] = total[:n].astype(bf16)
    rel_ref[:m, :] = total[n:]
    if rel_ref.shape[0] > m:
        rel_ref[m:, :] = jnp.zeros((rel_ref.shape[0] - m, LANES), f32)


def sum_pieces(x, packed, relrows):
    return pl.pallas_call(
        sum_kernel,
        out_shape=(
            jax.ShapeDtypeStruct((packed, LANES), bf16),
            jax.ShapeDtypeStruct((relrows, LANES), f32),
        ),
        compiler_params=pltpu.CompilerParams(vmem_limit_bytes=VMEM),
        name="sum_pieces",
    )(x)


def across(x, n):
    part = n // 8
    rest = x[3 * n : 3 * n + part].T
    rest = jnp.concatenate([rest[k * REST : (k + 1) * REST] for k in range(8)], axis=1)
    return jnp.concatenate([x[:n].T, x[n : 2 * n].T, x[2 * n : 3 * n].T, rest], axis=0)


def update_kernel(a_ref, b_ref, emb_ref, out_ref):
    width, n = emb_ref.shape
    g = jnp.sum(a_ref[...].astype(f32), axis=0) + b_ref[...].astype(f32)
    new = (emb_ref[...].astype(f32) - 0.5 * across(g, n)).astype(bf16)
    for i in range(n // LANES):
        out_ref[i * width : (i + 1) * width, :] = new[:, i * LANES : (i + 1) * LANES]


def update(a, b, emb):
    width, n = emb.shape
    return pl.pallas_call(
        update_kernel,
        out_shape=jax.ShapeDtypeStruct((width * n // LANES, LANES), bf16),
        compiler_params=pltpu.CompilerParams(vmem_limit_bytes=VMEM),
        name="update",
    )(a, b, emb)


def finish_kernel(x_ref, dirty_ref, up_ref, check_ref):
    width, n = up_ref.shape
    for i in range(n // LANES):
        at = slice(i * LANES, (i + 1) * LANES)
        x = x_ref[0, i * width : (i + 1) * width, :]
        up_ref[:, at] = x
        check_ref[:, at] = jnp.where(dirty_ref[:, at] == 1, x.astype(f32), 0.0).astype(bf16)


def finish(x, dirty, width, rows):
    pieces, wire, _ = x.shape
    n = rows // pieces
    out = jax.ShapeDtypeStruct((width, rows), bf16)
    return pl.pallas_call(
        finish_kernel,
        grid=(pieces,),
        in_specs=[
            pl.BlockSpec((1, wire, LANES), lambda i: (i, 0, 0)),
            pl.BlockSpec((1, n), lambda i: (0, i)),
        ],
        out_specs=[pl.BlockSpec((width, n), lambda i: (0, i))] * 2,
        out_shape=(out, out),
        compiler_params=pltpu.CompilerParams(vmem_limit_bytes=VMEM),
        name="finish",
    )(x, dirty)


def relation_kernel(m, x_ref, out_ref):
    cols = jnp.concatenate(
        [across(x_ref[i].astype(f32), m) for i in range(x_ref.shape[0])], axis=1
    )
    out_ref[...] = cols[:, : out_ref.shape[1]]


def relation_out(x, m, shape):
    return pl.pallas_call(
        functools.partial(relation_kernel, m),
        out_shape=jax.ShapeDtypeStruct(shape, f32),
        compiler_params=pltpu.CompilerParams(vmem_limit_bytes=VMEM),
        name="relation_out",
    )(x)


def to_all(x, axes, count):
    return lax.all_to_all(jnp.broadcast_to(x, (count,) + x.shape), axes, 0, 0, tiled=True)


def local(
    embeddings, relation, source_ids, relation_ids, target_ids, negative_ids, edge_counts, dirty
):
    rows, width = embeddings.shape
    nrel = relation.shape[0]
    group = ("side", "rep")
    doms = lax.axis_size("dom")
    count = edge_counts.reshape(1)
    nneg = negative_ids.shape[-1]
    src = source_ids.reshape(-1) * GROUPS
    rid = relation_ids.reshape(-1) * GROUPS
    dst = target_ids.reshape(-1) * GROUPS
    neg = (jnp.pad(negative_ids[0, 0, 0], ((0, 0), (0, SPAN - nneg))) * GROUPS).reshape(-1)
    me = lax.axis_index("side") * lax.axis_size("rep") + lax.axis_index("rep")
    piece = rows // PIECES
    own = lax.dynamic_slice_in_dim(embeddings.T, me * piece, piece, 1)

    dst_slab = shifted(embeddings, "dom", -1)
    e_rows, r_rows = edge_rows(count, src, rid, embeddings, relation)
    sent, values = edge_blocks(nneg, count, rid, dst, neg, dst_slab, e_rows, r_rows, nrel)
    got = lax.all_to_all(sent, group, 0, 0, tiled=True)
    gsrc = source_rows(count, src, values, rows)

    packed = gsrc.shape[1]
    relrows = -(-(sent.shape[1] - packed) // (8 * doms)) * 8 * doms
    gdst, rel = sum_pieces(got, packed, relrows)
    returned = shifted(gdst, "dom", 1)
    rel = lax.all_to_all(rel.reshape(doms, -1, LANES), "dom", 0, 0, tiled=True)
    rel = to_all(jnp.sum(rel, axis=0).astype(bf16), "dom", doms).reshape(-1, LANES)
    a = lax.all_to_all(gsrc, group, 0, 0, tiled=True)
    mine = update(a, returned, own)
    every = to_all(jnp.concatenate([mine, rel], axis=0), group, PIECES)
    updated, checkpoint = finish(every[:, : mine.shape[0]], dirty[None, :], width, rows)
    relm = -(-nrel // (PIECES * 64)) * 64
    relation_grad = relation_out(every[:, mine.shape[0] :], relm, (width, nrel))
    return (updated.T, relation_grad.T, checkpoint.T)


def solution(mesh):
    placed = (
        P("dom", None),
        P(),
        P("dom", "side", "rep", None),
        P("dom", "side", "rep", None),
        P("dom", "side", "rep", None),
        P("dom", "side", "rep", None, None),
        P("dom", "side", "rep"),
        P("dom"),
    )
    return jax.shard_map(
        local,
        mesh=mesh,
        in_specs=placed,
        out_specs=(P("dom", None), P(), P("dom", None)),
        check_vma=False,
    )
```

```python
import functools

import jax
import jax.numpy as jnp
from jax import lax
from jax.experimental import pallas as pl
from jax.experimental.pallas import tpu as pltpu
from jax.sharding import PartitionSpec as P

SPAN = 1024
LANES = 128
GROUPS = 4
REST = 16
FLAT = SPAN * GROUPS
CHUNK = 256
PIECES = 8
VMEM = 61 * 2**20

f32 = jnp.float32
bf16 = jnp.bfloat16


def shifted(x, axis, by):
    count = lax.axis_size(axis)
    return lax.ppermute(x, axis, [(i, (i + by) % count) for i in range(count)])


def row_of(index):
    return pl.ds(pl.multiple_of(index, GROUPS), GROUPS)


def slot_of(base, k):
    return pl.ds(base + (k // 8) * 8 * GROUPS + k % 8, GROUPS, stride=8)


def tiles(x):
    n = x.shape[0] // GROUPS
    x = x.reshape(n // 8, GROUPS, 8, LANES)
    return [x[:, c].reshape(n, LANES) for c in range(GROUPS)]


def untiles(cols):
    n = cols[0].shape[0]
    x = jnp.concatenate([c.reshape(n // 8, 1, 8, LANES) for c in cols], axis=1)
    return x.reshape(n * GROUPS, LANES)


def fill_rows(x, table, first, n):
    x = x.astype(f32)
    for c in range(GROUPS):
        part = x[:, c * LANES : min((c + 1) * LANES, x.shape[1])]
        if part.shape[1] < LANES:
            part = jnp.concatenate(
                [part, jnp.zeros((n, LANES - part.shape[1]), f32)], axis=1
            )
        table[pl.ds(first * GROUPS + c, n, stride=GROUPS), :] = part


def load_table(src_hbm, raw, sems, table):
    part = raw.shape[1]
    count = src_hbm.shape[0] // part

    def copy(i, slot):
        return pltpu.make_async_copy(
            src_hbm.at[pl.ds(pl.multiple_of(i * part, part), part)], raw.at[slot], sems.at[slot]
        )

    for i in range(2):
        copy(i, i).start()

    @pl.loop(0, count)
    def _(i):
        slot = lax.rem(i, 2)
        copy(i, slot).wait()

        @pl.loop(0, part // 64)
        def _(q):
            at = pl.multiple_of(q * 64, 64)
            fill_rows(raw[slot, pl.ds(at, 64), :], table, i * part + at, 64)

        @pl.when(i + 2 < count)
        def _():
            copy(i + 2, slot).start()


def edge_rows_kernel(count, src_i, rid_i, emb_hbm, rel_ref, e_out, r_out, ts, tr, raw, eb, rb, lsem, sems):
    load_table(emb_hbm, raw, lsem, ts)
    nrel = rel_ref.shape[0]
    whole = nrel // 64

    @pl.loop(0, whole)
    def _(q):
        first = pl.multiple_of(q * 64, 64)
        fill_rows(rel_ref[pl.ds(first, 64), :], tr, first, 64)

    for i in range(whole * 64, nrel):
        fill_rows(rel_ref[i : i + 1, :], tr, i, 1)

    nblocks = (count[0] + SPAN - 1) // SPAN

    def copies(blk, slot):
        return (
            pltpu.make_async_copy(eb.at[slot], e_out.at[blk], sems.at[slot, 0]),
            pltpu.make_async_copy(rb.at[slot], r_out.at[blk], sems.at[slot, 1]),
        )

    def step(blk, _):
        slot = lax.rem(blk, 2)

        @pl.when(blk >= 2)
        def _():
            for c in copies(blk - 2, slot):
                c.wait()

        es, rs = eb.at[slot], rb.at[slot]

        @pl.loop(0, SPAN // 16)
        def _(q):
            base = pl.multiple_of(q * 16 * GROUPS, 64)
            for k in range(16):
                j = blk * SPAN + q * 16 + k
                es[slot_of(base, k), :] = ts[row_of(src_i[j]), :]
                rs[slot_of(base, k), :] = tr[row_of(rid_i[j]), :]

        for c in copies(blk, slot):
            c.start()
        return 0

    lax.fori_loop(0, nblocks, step, 0)

    @pl.when(nblocks >= 2)
    def _():
        for c in copies(nblocks - 2, lax.rem(nblocks, 2)):
            c.wait()

    for c in copies(nblocks - 1, lax.rem(nblocks + 1, 2)):
        c.wait()


def write_piece(first, n, load, stage):
    for c in range(GROUPS - 1):
        stage[c * n : (c + 1) * n, :] = load(c, first, n).astype(stage.dtype)
    part = n // 8
    rest = load(GROUPS - 1, first, part)
    for k in range(1, 8):
        rest = rest + pltpu.roll(load(GROUPS - 1, first + k * part, part), k * REST, 1)
    stage[3 * n : 3 * n + part, :] = rest.astype(stage.dtype)


def zero(acc):
    n = acc.shape[0]
    whole = n // 256

    @pl.loop(0, whole)
    def _(q):
        acc[pl.ds(pl.multiple_of(q * 256, 256), 256), :] = jnp.zeros((256, LANES), f32)

    if n % 256:
        acc[whole * 256 :, :] = jnp.zeros((n - whole * 256, LANES), f32)


def add_rows(ops):
    values = [val[at, :] for _, _, val, at in ops]
    held = [acc[row, :] for acc, row, _, _ in ops]
    for (acc, row, _, _), v, h in zip(ops, values, held):
        acc[row, :] = h + v


def plane(accs):
    def load(c, first, n):
        at = pl.ds(first * GROUPS + c, n, stride=GROUPS)
        x = accs[0][at, :]
        for acc in accs[1:]:
            x = x + acc[at, :]
        return x

    return load


def block_kernel(
    nneg, count, rid_i, dst_i, neg_i, dst_hbm, e_hbm, r_hbm,
    lo_out, hi_out, rel_out, v_out,
    td, a0, a1, a2, r0_acc, r1_acc, raw, eb, rb, db, nb, lb, nbb, dn, stage, rstage, lsem, sems, vsem, osem,
):
    total = count[0]
    nblocks = (total + SPAN - 1) // SPAN

    def fetches(blk, slot):
        return (
            pltpu.make_async_copy(e_hbm.at[blk], eb.at[slot], sems.at[slot, 0]),
            pltpu.make_async_copy(r_hbm.at[blk], rb.at[slot], sems.at[slot, 1]),
        )

    def put(blk, slot):
        return pltpu.make_async_copy(rb.at[slot], v_out.at[blk], vsem.at[slot])

    for c in fetches(0, 0):
        c.start()
    load_table(dst_hbm, raw, lsem, td)
    for acc in (a0, a1, a2, r0_acc, r1_acc):
        zero(acc)

    def step(blk, _):
        slot = lax.rem(blk, 2)

        @pl.when(blk >= 1)
        def _():
            put(blk - 1, 1 - slot).wait()

        @pl.when(blk + 1 < nblocks)
        def _():
            for c in fetches(blk + 1, 1 - slot):
                c.start()

        first = blk * SPAN
        es, rs = eb.at[slot], rb.at[slot]

        @pl.loop(0, SPAN // 16)
        def _(q):
            base = pl.multiple_of(q * 16 * GROUPS, 64)
            for k in range(16):
                j = first + q * 16 + k
                db[slot_of(base, k), :] = td[row_of(dst_i[j]), :]
                nb[slot_of(base, k), :] = td[row_of(neg_i[j]), :]

        for ch in range(SPAN // CHUNK):
            cols = tiles(nb[ch * CHUNK * GROUPS : (ch + 1) * CHUNK * GROUPS, :])
            for c in range(GROUPS):
                nbb[ch * CHUNK : (ch + 1) * CHUNK, c * LANES : (c + 1) * LANES] = cols[c].astype(bf16)

        for c in fetches(blk, slot):
            c.wait()

        @pl.loop(0, SPAN // CHUNK)
        def _(ch):
            r0 = pl.multiple_of(ch * CHUNK, CHUNK)
            flat = pl.ds(pl.multiple_of(ch * CHUNK * GROUPS, CHUNK * GROUPS), CHUNK * GROUPS)
            e = tiles(es[flat, :])
            r = tiles(rs[flat, :])
            d = tiles(db[flat, :])
            left = [(e[c] * r[c]).astype(bf16) for c in range(GROUPS)]
            leftf = [x.astype(f32) for x in left]
            prod = leftf[0] * d[0]
            for c in range(1, GROUPS):
                prod = prod + leftf[c] * d[c]
            positive = jnp.sum(prod, axis=1, keepdims=True)
            lc = jnp.concatenate(left, axis=1)
            lb[pl.ds(r0, CHUNK), :] = lc
            negative = lax.dot_general(
                lc, nbb[...], (((1,), (1,)), ((), ())), preferred_element_type=f32
            )
            lane = lax.broadcasted_iota(jnp.int32, negative.shape, 1)
            negative = jnp.where(lane < nneg, negative, -jnp.inf)
            top = jnp.maximum(positive, jnp.max(negative, axis=1, keepdims=True))
            e_pos = jnp.exp(positive - top)
            e_neg = jnp.exp(negative - top)
            z = e_pos + jnp.sum(e_neg, axis=1, keepdims=True)
            row = lax.broadcasted_iota(jnp.int32, (CHUNK, 1), 0) + (first + r0)
            live = jnp.where(row < total, 1.0, 0.0).astype(f32)
            inv = 1.0 / z
            d_pos = live * (e_pos * inv - 1.0)
            d_neg = (e_neg * (live * inv)).astype(bf16)
            dn[pl.ds(r0, CHUNK), :] = d_neg
            dl = jnp.dot(d_neg, nbb[...], preferred_element_type=f32)
            x = [d_pos * d[c] + dl[:, c * LANES : (c + 1) * LANES] for c in range(GROUPS)]
            db[flat, :] = untiles([d_pos * leftf[c] for c in range(GROUPS)])
            es[flat, :] = untiles([x[c] * e[c] for c in range(GROUPS)])
            rs[flat, :] = untiles([x[c] * r[c] for c in range(GROUPS)])

        put(blk, slot).start()

        for ch in range(SPAN // CHUNK):
            part = lax.dot_general(
                dn[:, ch * CHUNK : (ch + 1) * CHUNK], lb[...], (((0,), (0,)), ((), ())),
                preferred_element_type=f32,
            )
            nb[ch * CHUNK * GROUPS : (ch + 1) * CHUNK * GROUPS, :] = untiles(
                [part[:, c * LANES : (c + 1) * LANES] for c in range(GROUPS)]
            )

        def scatter(j0, base, n):
            for t in range(0, n, 3):
                ks = list(range(t, min(t + 3, n)))
                at = [slot_of(base, k) for k in ks]
                copies = (a0, a1, a2)
                dst = [(copies[i], row_of(dst_i[j0 + k]), db, at[i]) for i, k in enumerate(ks)]
                neg = [(copies[i], row_of(neg_i[j0 + k]), nb, at[i]) for i, k in enumerate(ks)]
                rel = [
                    ((r0_acc, r1_acc)[i % 2], row_of(rid_i[j0 + k]), es, at[i])
                    for i, k in enumerate(ks)
                ]
                add_rows(dst + rel[:2])
                add_rows(neg + rel[2:])

        @pl.loop(0, SPAN // 24)
        def _(q):
            scatter(first + q * 24, pl.multiple_of(q * 24 * GROUPS, 32), 24)

        done = SPAN // 24 * 24
        scatter(first + done, done * GROUPS, SPAN - done)
        return 0

    lax.fori_loop(0, nblocks, step, 0)
    last = nblocks - 1
    put(last, lax.rem(last, 2)).wait()

    m = r0_acc.shape[0] // GROUPS // PIECES
    packed = m * 25 // 8
    grad, rel = plane((a0, a1, a2)), plane((r0_acc, r1_acc))

    def fill_rel(j, st):
        write_piece(j * m, m, rel, st)
        if st.shape[0] > packed:
            st[packed:, :] = jnp.zeros((st.shape[0] - packed, LANES), st.dtype)

    emit_halves(grad, td.shape[0] // GROUPS, lo_out, hi_out, stage, osem)
    emit(fill_rel, rel_out, rstage, osem)


def emit(fill, out, stage, sem):
    def copy(j, slot):
        return pltpu.make_async_copy(stage.at[slot], out.at[j], sem.at[slot])

    @pl.loop(0, PIECES)
    def _(j):
        slot = lax.rem(j, 2)

        @pl.when(j >= 2)
        def _():
            copy(j - 2, slot).wait()

        fill(j, stage.at[slot])
        copy(j, slot).start()

    for j in (PIECES - 2, PIECES - 1):
        copy(j, j % 2).wait()


def emit_halves(load, rows, lo_out, hi_out, stage, sem):
    half = rows // PIECES // 2
    for h, out in enumerate((lo_out, hi_out)):
        emit(
            lambda j, st, h=h: write_piece((2 * j + h) * half, half, load, st), out, stage, sem
        )


def source_kernel(count, src_i, v_hbm, lo_out, hi_out, a0, a1, a2, a3, vb, stage, sems, osem):
    nblocks = (count[0] + SPAN - 1) // SPAN
    accs = (a0, a1, a2, a3)

    def fetch(blk, slot):
        return pltpu.make_async_copy(v_hbm.at[blk], vb.at[slot], sems.at[slot])

    fetch(0, 0).start()
    for acc in accs:
        zero(acc)

    def step(blk, _):
        slot = lax.rem(blk, 2)

        @pl.when(blk + 1 < nblocks)
        def _():
            fetch(blk + 1, 1 - slot).start()

        fetch(blk, slot).wait()
        vs = vb.at[slot]

        @pl.loop(0, SPAN // 16)
        def _(q):
            base = pl.multiple_of(q * 16 * GROUPS, 64)
            for t in range(0, 16, 4):
                add_rows(
                    [
                        (accs[i], row_of(src_i[blk * SPAN + q * 16 + t + i]), vs, slot_of(base, t + i))
                        for i in range(4)
                    ]
                )

        return 0

    lax.fori_loop(0, nblocks, step, 0)
    emit_halves(plane(accs), a0.shape[0] // GROUPS, lo_out, hi_out, stage, osem)


def smem():
    return pl.BlockSpec(memory_space=pltpu.SMEM)


def hbm():
    return pl.BlockSpec(memory_space=pl.ANY)


def edge_rows(count, src, rid, emb, relation):
    nb = src.shape[0] // SPAN
    rows = emb.shape[0]
    nrel = relation.shape[0]
    shape = jax.ShapeDtypeStruct((nb, FLAT, LANES), f32)
    return pl.pallas_call(
        edge_rows_kernel,
        out_shape=(shape, shape),
        in_specs=[smem()] * 3 + [hbm(), pl.BlockSpec(memory_space=pltpu.VMEM)],
        out_specs=(hbm(), hbm()),
        scratch_shapes=[
            pltpu.VMEM((rows * GROUPS, LANES), f32),
            pltpu.VMEM((-(-nrel // 8) * 8 * GROUPS, LANES), f32),
            pltpu.VMEM((2, 512, emb.shape[1]), bf16),
            pltpu.VMEM((2, FLAT, LANES), f32),
            pltpu.VMEM((2, FLAT, LANES), f32),
            pltpu.SemaphoreType.DMA((2,)),
            pltpu.SemaphoreType.DMA((2, 2)),
        ],
        compiler_params=pltpu.CompilerParams(vmem_limit_bytes=VMEM),
        cost_estimate=pl.CostEstimate(flops=0, bytes_accessed=60_000_000, transcendentals=0),
        name="edge_rows",
    )(count, src, rid, emb, relation)


def edge_blocks(nneg, count, rid, dst, neg, dst_slab, e_rows, r_rows, nrel):
    rows = dst_slab.shape[0]
    packed = rows // PIECES // 2 * 25 // 8
    half = jax.ShapeDtypeStruct((PIECES, packed, LANES), bf16)
    relm = -(-nrel // (PIECES * 64)) * 64
    relrows = -(-(relm * 25 // 8) // 128) * 128
    table = pltpu.VMEM((rows * GROUPS, LANES), f32)
    rel = pltpu.VMEM((relm * PIECES * GROUPS, LANES), f32)
    return pl.pallas_call(
        functools.partial(block_kernel, nneg),
        out_shape=(
            half,
            half,
            jax.ShapeDtypeStruct((PIECES, relrows, LANES), bf16),
            jax.ShapeDtypeStruct(r_rows.shape, f32),
        ),
        in_specs=[smem()] * 4 + [hbm()] * 3,
        out_specs=(hbm(), hbm(), hbm(), hbm()),
        scratch_shapes=[
            table, table, table, table, rel, rel,
            pltpu.VMEM((2, 512, dst_slab.shape[1]), bf16),
            pltpu.VMEM((2, FLAT, LANES), f32),
            pltpu.VMEM((2, FLAT, LANES), f32),
            pltpu.VMEM((FLAT, LANES), f32),
            pltpu.VMEM((FLAT, LANES), f32),
            pltpu.VMEM((SPAN, LANES * GROUPS), bf16),
            pltpu.VMEM((SPAN, LANES * GROUPS), bf16),
            pltpu.VMEM((SPAN, SPAN), bf16),
            pltpu.VMEM((2, packed, LANES), bf16),
            pltpu.VMEM((2, relrows, LANES), bf16),
            pltpu.SemaphoreType.DMA((2,)),
            pltpu.SemaphoreType.DMA((2, 2)),
            pltpu.SemaphoreType.DMA((2,)),
            pltpu.SemaphoreType.DMA((2,)),
        ],
        compiler_params=pltpu.CompilerParams(vmem_limit_bytes=VMEM),
        name="edge_blocks",
    )(count, rid, dst, neg, dst_slab, e_rows, r_rows)


def source_rows(count, src, values, rows):
    packed = rows // PIECES // 2 * 25 // 8
    half = jax.ShapeDtypeStruct((PIECES, packed, LANES), bf16)
    table = pltpu.VMEM((rows * GROUPS, LANES), f32)
    return pl.pallas_call(
        source_kernel,
        out_shape=(half, half),
        in_specs=[smem()] * 2 + [hbm()],
        out_specs=(hbm(), hbm()),
        scratch_shapes=[
            table, table, table, table,
            pltpu.VMEM((2, FLAT, LANES), f32),
            pltpu.VMEM((2, packed, LANES), bf16),
            pltpu.SemaphoreType.DMA((2,)),
            pltpu.SemaphoreType.DMA((2,)),
        ],
        compiler_params=pltpu.CompilerParams(vmem_limit_bytes=VMEM),
        cost_estimate=pl.CostEstimate(flops=0, bytes_accessed=60_000_000, transcendentals=0),
        name="source_rows",
    )(count, src, values)


def sum_kernel(x_ref, after_ref, out_ref):
    out_ref[...] = jnp.sum(x_ref[...].astype(f32), axis=0)


def sum_pieces(x, after):
    return pl.pallas_call(
        sum_kernel,
        out_shape=jax.ShapeDtypeStruct(x.shape[1:], f32),
        in_specs=[pl.BlockSpec(memory_space=pltpu.VMEM), hbm()],
        compiler_params=pltpu.CompilerParams(vmem_limit_bytes=VMEM),
        name="sum_pieces",
    )(x, after)


def across(x, n):
    part = n // 8
    rest = x[3 * n : 3 * n + part].T
    rest = jnp.concatenate([rest[k * REST : (k + 1) * REST] for k in range(8)], axis=1)
    return jnp.concatenate([x[:n].T, x[n : 2 * n].T, x[2 * n : 3 * n].T, rest], axis=0)


def update_kernel(a_ref, emb_ref, out_ref):
    width, n = emb_ref.shape
    g = jnp.sum(a_ref[...].astype(f32), axis=0)
    new = (emb_ref[...].astype(f32) - 0.5 * across(g, n)).astype(bf16)
    for i in range(n // LANES):
        out_ref[i * width : (i + 1) * width, :] = new[:, i * LANES : (i + 1) * LANES]


def update(a, emb):
    width, n = emb.shape
    return pl.pallas_call(
        update_kernel,
        out_shape=jax.ShapeDtypeStruct((width * n // LANES, LANES), bf16),
        compiler_params=pltpu.CompilerParams(vmem_limit_bytes=VMEM),
        name="update",
    )(a, emb)


def finish_kernel(place, a_ref, ar_ref, b0_ref, b1_ref, b2_ref, b3_ref, dirty_ref, up_ref, check_ref):
    width = up_ref.shape[0]
    half = dirty_ref.shape[1] // PIECES // 2
    blocks = [(a_ref, k, k, 0) for k in range(4)] + [(ar_ref, k, 4 + k, 0) for k in range(4)]
    for k, ref in enumerate((b0_ref, b1_ref, b2_ref, b3_ref)):
        blocks += [(ref, 0, k, half), (ref, 1, 4 + k, half)]
    for ref, i, at_place, off in blocks:
        start = pl.multiple_of(place[at_place] * 2 * half + off, half)
        for k in range(half // LANES):
            at = pl.ds(pl.multiple_of(start + k * LANES, LANES), LANES)
            x = ref[i, k * width : (k + 1) * width, :]
            up_ref[:, at] = x
            check_ref[:, at] = jnp.where(dirty_ref[:, at] == 1, x.astype(f32), 0.0).astype(bf16)


def finish(place, parts, dirty, width):
    out = jax.ShapeDtypeStruct((width, dirty.shape[1]), bf16)
    return pl.pallas_call(
        finish_kernel,
        in_specs=[smem()] + [pl.BlockSpec(memory_space=pltpu.VMEM)] * 7,
        out_shape=(out, out),
        compiler_params=pltpu.CompilerParams(vmem_limit_bytes=VMEM),
        name="finish",
    )(place, *parts, dirty)


def relation_kernel(m, order, x_ref, out_ref):
    cols = jnp.concatenate(
        [across(x_ref[order[i]].astype(f32), m) for i in range(PIECES)], axis=1
    )
    out_ref[...] = cols[:, : out_ref.shape[1]]


def relation_out(order, x, m, shape):
    return pl.pallas_call(
        functools.partial(relation_kernel, m),
        out_shape=jax.ShapeDtypeStruct(shape, f32),
        in_specs=[smem(), pl.BlockSpec(memory_space=pltpu.VMEM)],
        compiler_params=pltpu.CompilerParams(vmem_limit_bytes=VMEM),
        name="relation_out",
    )(order, x)


def around(x):
    return [x] + [shifted(x, "side", by) for by in (1, -1, 2)]


def both_reps(x):
    return [x, shifted(x, "rep", 1)]


def swapped(x, axis, bit):
    count = lax.axis_size(axis)
    return lax.ppermute(x, axis, [(i, i ^ bit) for i in range(count)])


def local(
    embeddings, relation, source_ids, relation_ids, target_ids, negative_ids, edge_counts, dirty
):
    rows, width = embeddings.shape
    nrel = relation.shape[0]
    group = ("side", "rep")
    doms = lax.axis_size("dom")
    count = edge_counts.reshape(1)
    nneg = negative_ids.shape[-1]
    src = source_ids.reshape(-1) * GROUPS
    rid = relation_ids.reshape(-1) * GROUPS
    dst = target_ids.reshape(-1) * GROUPS
    neg = (jnp.pad(negative_ids[0, 0, 0], ((0, 0), (0, SPAN - nneg))) * GROUPS).reshape(-1)
    me = lax.axis_index("side") * lax.axis_size("rep") + lax.axis_index("rep")
    piece = rows // PIECES
    half = piece // 2
    own = [lax.dynamic_slice_in_dim(embeddings.T, me * piece + h * half, half, 1) for h in (0, 1)]
    side, rep = lax.axis_index("side"), lax.axis_index("rep")
    sides = jnp.stack([side, (side + 3) % 4, (side + 1) % 4, (side + 2) % 4])
    place = jnp.concatenate([sides * 2 + rep, sides * 2 + 1 - rep]).astype(jnp.int32)
    order = jnp.argsort(place).astype(jnp.int32)

    dst_slab = shifted(embeddings, "dom", -1)
    e_rows, r_rows = edge_rows(count, src, rid, embeddings, relation)
    *gdst, grel, values = edge_blocks(nneg, count, rid, dst, neg, dst_slab, e_rows, r_rows, nrel)
    returned = [shifted(g, "dom", 1) for g in gdst]
    rel = lax.all_to_all(grel, group, 0, 0, tiled=True)
    gsrc = source_rows(count, src, values, rows)
    rel = sum_pieces(rel, gsrc[0])
    bit = 1
    while bit < doms:
        rel = rel + swapped(rel, "dom", bit)
        bit *= 2
    rel = jnp.concatenate(around(jnp.stack(both_reps(rel.astype(bf16)))))
    relm = -(-nrel // (PIECES * 64)) * 64
    rel_order = (order % 4) * 2 + order // 4
    relation_grad = relation_out(rel_order, rel, relm, (width, nrel))

    mine = [
        update(lax.all_to_all(gsrc[h] + returned[h], group, 0, 0, tiled=True), own[h])
        for h in (0, 1)
    ]
    a4 = jnp.stack(around(mine[0]))
    parts = both_reps(a4) + around(jnp.stack(both_reps(mine[1])))
    updated, checkpoint = finish(place, parts, dirty[None, :], width)
    return (updated.T, relation_grad.T, checkpoint.T)


def solution(mesh):
    placed = (
        P("dom", None),
        P(),
        P("dom", "side", "rep", None),
        P("dom", "side", "rep", None),
        P("dom", "side", "rep", None),
        P("dom", "side", "rep", None, None),
        P("dom", "side", "rep"),
        P("dom"),
    )
    return jax.shard_map(
        local,
        mesh=mesh,
        in_specs=placed,
        out_specs=(P("dom", None), P(), P("dom", None)),
        check_vma=False,
    )
```

```python
import functools

import jax
import jax.numpy as jnp
from jax import lax
from jax.experimental import pallas as pl
from jax.experimental.pallas import tpu as pltpu
from jax.sharding import PartitionSpec as P

SPAN = 1024
LANES = 128
GROUPS = 4
REST = 16
FLAT = SPAN * GROUPS
CHUNK = SPAN // 2
HALF = FLAT // 2
PIECES = 8
SLOTS = 4
VMEM = 61 * 2**20

f32 = jnp.float32
bf16 = jnp.bfloat16


def shifted(x, axis, by):
    count = lax.axis_size(axis)
    return lax.ppermute(x, axis, [(i, (i + by) % count) for i in range(count)])


def row_of(index):
    return pl.ds(pl.multiple_of(index, GROUPS), GROUPS)


def slot_of(base, k):
    return pl.ds(base + (k // 8) * 8 * GROUPS + k % 8, GROUPS, stride=8)


def tiles(x):
    n = x.shape[0] // GROUPS
    x = x.reshape(n // 8, GROUPS, 8, LANES)
    return [x[:, c].reshape(n, LANES) for c in range(GROUPS)]


def untiles(cols):
    n = cols[0].shape[0]
    x = jnp.concatenate([c.reshape(n // 8, 1, 8, LANES) for c in cols], axis=1)
    return x.reshape(n * GROUPS, LANES)


def gather_rows(ops, base, n):
    for k0 in range(0, n, 8):
        ks = range(k0, k0 + 8)
        held = [[table[row_of(ids[j + k]), :] for table, ids, j, _ in ops] for k in ks]
        for k, rows in zip(ks, held):
            for (_, _, _, out), x in zip(ops, rows):
                out[slot_of(base, k), :] = x


def fill_rows(x, table, first, n):
    x = x.astype(f32)
    for c in range(GROUPS):
        part = x[:, c * LANES : min((c + 1) * LANES, x.shape[1])]
        if part.shape[1] < LANES:
            part = jnp.concatenate(
                [part, jnp.zeros((n, LANES - part.shape[1]), f32)], axis=1
            )
        table[pl.ds(first * GROUPS + c, n, stride=GROUPS), :] = part


def load_table(src_hbm, raw, sems, table):
    part = raw.shape[1]
    count = src_hbm.shape[0] // part

    def copy(i, slot):
        return pltpu.make_async_copy(
            src_hbm.at[pl.ds(pl.multiple_of(i * part, part), part)], raw.at[slot], sems.at[slot]
        )

    for i in range(2):
        copy(i, i).start()

    @pl.loop(0, count)
    def _(i):
        slot = lax.rem(i, 2)
        copy(i, slot).wait()

        @pl.loop(0, part // 64)
        def _(q):
            at = pl.multiple_of(q * 64, 64)
            fill_rows(raw[slot, pl.ds(at, 64), :], table, i * part + at, 64)

        @pl.when(i + 2 < count)
        def _():
            copy(i + 2, slot).start()


def edge_rows_kernel(
    count, src_i, rid_i, emb_hbm, rel_ref, e_out, r_out, ts, tr, raw, eb0, eb1, rb0, rb1, lsem, sems
):
    load_table(emb_hbm, raw, lsem, ts)
    nrel = rel_ref.shape[0]
    whole = nrel // 64

    @pl.loop(0, whole)
    def _(q):
        first = pl.multiple_of(q * 64, 64)
        fill_rows(rel_ref[pl.ds(first, 64), :], tr, first, 64)

    for i in range(whole * 64, nrel):
        fill_rows(rel_ref[i : i + 1, :], tr, i, 1)

    nblocks = (count[0] + SPAN - 1) // SPAN
    outs = ((eb0, e_out, 0), (eb1, e_out, 1), (rb0, r_out, 0), (rb1, r_out, 1))

    def copies(blk, slot):
        return [
            pltpu.make_async_copy(
                buf.at[slot], out.at[blk, pl.ds(h * HALF, HALF)], sems.at[slot, i]
            )
            for i, (buf, out, h) in enumerate(outs)
        ]

    def step(blk, _):
        slot = lax.rem(blk, 2)

        @pl.when(blk >= 2)
        def _():
            for c in copies(blk - 2, slot):
                c.wait()

        e0, e1, r0, r1 = (x.at[slot] for x in (eb0, eb1, rb0, rb1))

        @pl.loop(0, SPAN // 32)
        def _(q):
            base = pl.multiple_of(q * 16 * GROUPS, 64)
            j = blk * SPAN + q * 16
            gather_rows(
                [
                    (ts, src_i, j, e0),
                    (ts, src_i, j + SPAN // 2, e1),
                    (tr, rid_i, j, r0),
                    (tr, rid_i, j + SPAN // 2, r1),
                ],
                base,
                16,
            )

        for c in copies(blk, slot):
            c.start()
        return 0

    lax.fori_loop(0, nblocks, step, 0)

    @pl.when(nblocks >= 2)
    def _():
        for c in copies(nblocks - 2, lax.rem(nblocks, 2)):
            c.wait()

    for c in copies(nblocks - 1, lax.rem(nblocks + 1, 2)):
        c.wait()


def write_piece(first, n, load, stage):
    for c in range(GROUPS - 1):
        stage[c * n : (c + 1) * n, :] = load(c, first, n).astype(stage.dtype)
    part = n // 8
    rest = load(GROUPS - 1, first, part)
    for k in range(1, 8):
        rest = rest + pltpu.roll(load(GROUPS - 1, first + k * part, part), k * REST, 1)
    stage[3 * n : 3 * n + part, :] = rest.astype(stage.dtype)


def zero(acc):
    n = acc.shape[0]
    whole = n // 256

    @pl.loop(0, whole)
    def _(q):
        acc[pl.ds(pl.multiple_of(q * 256, 256), 256), :] = jnp.zeros((256, LANES), f32)

    if n % 256:
        acc[whole * 256 :, :] = jnp.zeros((n - whole * 256, LANES), f32)


def add_rows(ops):
    values = [val[at, :] for _, _, val, at in ops]
    held = [acc[row, :] for acc, row, _, _ in ops]
    for (acc, row, _, _), v, h in zip(ops, values, held):
        acc[row, :] = h + v


def plane(accs):
    def load(c, first, n):
        at = pl.ds(first * GROUPS + c, n, stride=GROUPS)
        x = accs[0][at, :]
        for acc in accs[1:]:
            x = x + acc[at, :]
        return x

    return load


def block_kernel(
    nneg, count, rid_i, dst_i, neg_i, dst_hbm, e_hbm, r_hbm,
    lo_out, hi_out, rel_out, v_out,
    td, a0, a1, a2, r0_acc, r1_acc, raw, eb, rb, db0, db1, nb0, nb1, lb, nbb, dn, stage, rstage, lsem, sems, vsem, osem,
):
    total = count[0]
    nblocks = (total + SPAN - 1) // SPAN

    def fetches(blk, slot):
        return (
            pltpu.make_async_copy(e_hbm.at[blk], eb.at[slot], sems.at[slot, 0]),
            pltpu.make_async_copy(r_hbm.at[blk], rb.at[slot], sems.at[slot, 1]),
        )

    def put(blk, slot):
        return pltpu.make_async_copy(rb.at[slot], v_out.at[blk], vsem.at[slot])

    for c in fetches(0, 0):
        c.start()
    load_table(dst_hbm, raw, lsem, td)
    for acc in (a0, a1, a2, r0_acc, r1_acc):
        zero(acc)

    def step(blk, _):
        slot = lax.rem(blk, 2)

        @pl.when(blk >= 1)
        def _():
            put(blk - 1, 1 - slot).wait()

        @pl.when(blk + 1 < nblocks)
        def _():
            for c in fetches(blk + 1, 1 - slot):
                c.start()

        first = blk * SPAN
        es, rs = eb.at[slot], rb.at[slot]

        @pl.loop(0, SPAN // 32)
        def _(q):
            base = pl.multiple_of(q * 16 * GROUPS, 64)
            j = first + q * 16
            gather_rows(
                [
                    (td, dst_i, j, db0),
                    (td, dst_i, j + CHUNK, db1),
                    (td, neg_i, j, nb0),
                    (td, neg_i, j + CHUNK, nb1),
                ],
                base,
                16,
            )

        for ch, nb in enumerate((nb0, nb1)):
            cols = tiles(nb[...])
            for c in range(GROUPS):
                nbb[ch * CHUNK : (ch + 1) * CHUNK, c * LANES : (c + 1) * LANES] = cols[c].astype(bf16)

        for c in fetches(blk, slot):
            c.wait()

        for ch, db in enumerate((db0, db1)):
            r0 = ch * CHUNK
            flat = pl.ds(ch * HALF, HALF)
            e = tiles(es[flat, :])
            r = tiles(rs[flat, :])
            d = tiles(db[...])
            left = [(e[c] * r[c]).astype(bf16) for c in range(GROUPS)]
            leftf = [x.astype(f32) for x in left]
            prod = leftf[0] * d[0]
            for c in range(1, GROUPS):
                prod = prod + leftf[c] * d[c]
            positive = jnp.sum(prod, axis=1, keepdims=True)
            lc = jnp.concatenate(left, axis=1)
            lb[pl.ds(r0, CHUNK), :] = lc
            negative = lax.dot_general(
                lc, nbb[...], (((1,), (1,)), ((), ())), preferred_element_type=f32
            )
            edge = nneg // LANES * LANES
            lane = lax.broadcasted_iota(jnp.int32, (CHUNK, SPAN - edge), 1)
            negative = jnp.concatenate(
                [negative[:, :edge], jnp.where(lane < nneg - edge, negative[:, edge:], -jnp.inf)], axis=1
            )
            top = jnp.maximum(positive, jnp.max(negative, axis=1, keepdims=True))
            e_pos = jnp.exp(positive - top)
            e_neg = jnp.exp(negative - top)
            z = e_pos + jnp.sum(e_neg, axis=1, keepdims=True)
            row = lax.broadcasted_iota(jnp.int32, (CHUNK, 1), 0) + (first + r0)
            live = jnp.where(row < total, 1.0, 0.0).astype(f32)
            inv = 1.0 / z
            d_pos = live * (e_pos * inv - 1.0)
            d_neg = (e_neg * (live * inv)).astype(bf16)
            dn[pl.ds(r0, CHUNK), :] = d_neg
            dl = jnp.dot(d_neg, nbb[...], preferred_element_type=f32)
            x = [d_pos * d[c] + dl[:, c * LANES : (c + 1) * LANES] for c in range(GROUPS)]
            db[...] = untiles([d_pos * leftf[c] for c in range(GROUPS)])
            es[flat, :] = untiles([x[c] * e[c] for c in range(GROUPS)])
            rs[flat, :] = untiles([x[c] * r[c] for c in range(GROUPS)])

        put(blk, slot).start()

        for ch, nb in enumerate((nb0, nb1)):
            part = lax.dot_general(
                dn[:, ch * CHUNK : (ch + 1) * CHUNK], lb[...], (((0,), (0,)), ((), ())),
                preferred_element_type=f32,
            )
            nb[...] = untiles(
                [part[:, c * LANES : (c + 1) * LANES] for c in range(GROUPS)]
            )

        def scatter(h, start, base, n):
            db, nb, ev = ((db0, nb0), (db1, nb1))[h] + (es.at[pl.ds(h * HALF, HALF)],)
            j0 = first + h * CHUNK + start
            for t in range(0, n, 3):
                ks = list(range(t, min(t + 3, n)))
                at = [slot_of(base, k) for k in ks]
                copies = (a0, a1, a2)
                dst = [(copies[i], row_of(dst_i[j0 + k]), db, at[i]) for i, k in enumerate(ks)]
                neg = [(copies[i], row_of(neg_i[j0 + k]), nb, at[i]) for i, k in enumerate(ks)]
                rel = [
                    ((r0_acc, r1_acc)[i % 2], row_of(rid_i[j0 + k]), ev, at[i])
                    for i, k in enumerate(ks)
                ]
                add_rows(dst + rel[:2])
                add_rows(neg + rel[2:])

        for h in (0, 1):

            @pl.loop(0, CHUNK // 24)
            def _(q):
                scatter(h, q * 24, pl.multiple_of(q * 24 * GROUPS, 32), 24)

            done = CHUNK // 24 * 24
            scatter(h, done, done * GROUPS, CHUNK - done)
        return 0

    lax.fori_loop(0, nblocks, step, 0)
    last = nblocks - 1
    put(last, lax.rem(last, 2)).wait()

    m = r0_acc.shape[0] // GROUPS // PIECES
    packed = m * 25 // 8
    grad, rel = plane((a0, a1, a2)), plane((r0_acc, r1_acc))

    def fill_rel(j, st):
        write_piece(j * m, m, rel, st)
        if st.shape[0] > packed:
            st[packed:, :] = jnp.zeros((st.shape[0] - packed, LANES), st.dtype)

    emit_halves(grad, td.shape[0] // GROUPS, lo_out, hi_out, stage, osem)
    emit(fill_rel, rel_out, rstage, osem)


def emit(fill, out, stage, sem):
    def copy(j, slot):
        return pltpu.make_async_copy(stage.at[slot], out.at[j], sem.at[slot])

    @pl.loop(0, PIECES)
    def _(j):
        slot = lax.rem(j, SLOTS)

        @pl.when(j >= SLOTS)
        def _():
            copy(j - SLOTS, slot).wait()

        fill(j, stage.at[slot])
        copy(j, slot).start()

    for j in range(PIECES - SLOTS, PIECES):
        copy(j, j % SLOTS).wait()


def emit_halves(load, rows, lo_out, hi_out, stage, sem):
    half = rows // PIECES // 2
    for h, out in enumerate((lo_out, hi_out)):
        emit(
            lambda j, st, h=h: write_piece((2 * j + h) * half, half, load, st), out, stage, sem
        )


def source_kernel(count, src_i, v_hbm, lo_out, hi_out, a0, a1, a2, a3, vb, stage, sems, osem):
    nblocks = (count[0] + SPAN - 1) // SPAN
    accs = (a0, a1, a2, a3)

    def fetch(blk, slot):
        return pltpu.make_async_copy(v_hbm.at[blk], vb.at[slot], sems.at[slot])

    fetch(0, 0).start()
    for acc in accs:
        zero(acc)

    def step(blk, _):
        slot = lax.rem(blk, 2)

        @pl.when(blk + 1 < nblocks)
        def _():
            fetch(blk + 1, 1 - slot).start()

        fetch(blk, slot).wait()
        vs = vb.at[slot]

        @pl.loop(0, SPAN // 16)
        def _(q):
            base = pl.multiple_of(q * 16 * GROUPS, 64)
            for t in range(0, 16, 4):
                add_rows(
                    [
                        (accs[i], row_of(src_i[blk * SPAN + q * 16 + t + i]), vs, slot_of(base, t + i))
                        for i in range(4)
                    ]
                )

        return 0

    lax.fori_loop(0, nblocks, step, 0)
    emit_halves(plane(accs), a0.shape[0] // GROUPS, lo_out, hi_out, stage, osem)


def smem():
    return pl.BlockSpec(memory_space=pltpu.SMEM)


def hbm():
    return pl.BlockSpec(memory_space=pl.ANY)


def edge_rows(count, src, rid, emb, relation):
    nb = src.shape[0] // SPAN
    rows = emb.shape[0]
    nrel = relation.shape[0]
    shape = jax.ShapeDtypeStruct((nb, FLAT, LANES), f32)
    return pl.pallas_call(
        edge_rows_kernel,
        out_shape=(shape, shape),
        in_specs=[smem()] * 3 + [hbm(), pl.BlockSpec(memory_space=pltpu.VMEM)],
        out_specs=(hbm(), hbm()),
        scratch_shapes=[
            pltpu.VMEM((rows * GROUPS, LANES), f32),
            pltpu.VMEM((-(-nrel // 8) * 8 * GROUPS, LANES), f32),
            pltpu.VMEM((2, 512, emb.shape[1]), bf16),
            pltpu.VMEM((2, HALF, LANES), f32),
            pltpu.VMEM((2, HALF, LANES), f32),
            pltpu.VMEM((2, HALF, LANES), f32),
            pltpu.VMEM((2, HALF, LANES), f32),
            pltpu.SemaphoreType.DMA((2,)),
            pltpu.SemaphoreType.DMA((2, 4)),
        ],
        compiler_params=pltpu.CompilerParams(vmem_limit_bytes=VMEM),
        cost_estimate=pl.CostEstimate(flops=0, bytes_accessed=60_000_000, transcendentals=0),
        name="edge_rows",
    )(count, src, rid, emb, relation)


def edge_blocks(nneg, count, rid, dst, neg, dst_slab, e_rows, r_rows, nrel):
    rows = dst_slab.shape[0]
    packed = rows // PIECES // 2 * 25 // 8
    half = jax.ShapeDtypeStruct((PIECES, packed, LANES), bf16)
    relm = -(-nrel // (PIECES * 64)) * 64
    relrows = -(-(relm * 25 // 8) // 128) * 128
    table = pltpu.VMEM((rows * GROUPS, LANES), f32)
    rel = pltpu.VMEM((relm * PIECES * GROUPS, LANES), f32)
    return pl.pallas_call(
        functools.partial(block_kernel, nneg),
        out_shape=(
            half,
            half,
            jax.ShapeDtypeStruct((PIECES, relrows, LANES), bf16),
            jax.ShapeDtypeStruct(r_rows.shape, f32),
        ),
        in_specs=[smem()] * 4 + [hbm()] * 3,
        out_specs=(hbm(), hbm(), hbm(), hbm()),
        scratch_shapes=[
            table, table, table, table, rel, rel,
            pltpu.VMEM((2, 512, dst_slab.shape[1]), bf16),
            pltpu.VMEM((2, FLAT, LANES), f32),
            pltpu.VMEM((2, FLAT, LANES), f32),
            pltpu.VMEM((HALF, LANES), f32),
            pltpu.VMEM((HALF, LANES), f32),
            pltpu.VMEM((HALF, LANES), f32),
            pltpu.VMEM((HALF, LANES), f32),
            pltpu.VMEM((SPAN, LANES * GROUPS), bf16),
            pltpu.VMEM((SPAN, LANES * GROUPS), bf16),
            pltpu.VMEM((SPAN, SPAN), bf16),
            pltpu.VMEM((SLOTS, packed, LANES), bf16),
            pltpu.VMEM((SLOTS, relrows, LANES), bf16),
            pltpu.SemaphoreType.DMA((2,)),
            pltpu.SemaphoreType.DMA((2, 2)),
            pltpu.SemaphoreType.DMA((2,)),
            pltpu.SemaphoreType.DMA((SLOTS,)),
        ],
        compiler_params=pltpu.CompilerParams(vmem_limit_bytes=VMEM),
        name="edge_blocks",
    )(count, rid, dst, neg, dst_slab, e_rows, r_rows)


def source_rows(count, src, values, rows):
    packed = rows // PIECES // 2 * 25 // 8
    half = jax.ShapeDtypeStruct((PIECES, packed, LANES), bf16)
    table = pltpu.VMEM((rows * GROUPS, LANES), f32)
    return pl.pallas_call(
        source_kernel,
        out_shape=(half, half),
        in_specs=[smem()] * 2 + [hbm()],
        out_specs=(hbm(), hbm()),
        scratch_shapes=[
            table, table, table, table,
            pltpu.VMEM((2, FLAT, LANES), f32),
            pltpu.VMEM((SLOTS, packed, LANES), bf16),
            pltpu.SemaphoreType.DMA((2,)),
            pltpu.SemaphoreType.DMA((SLOTS,)),
        ],
        compiler_params=pltpu.CompilerParams(vmem_limit_bytes=VMEM),
        cost_estimate=pl.CostEstimate(flops=0, bytes_accessed=60_000_000, transcendentals=0),
        name="source_rows",
    )(count, src, values)


def sum_kernel(rep, x_ref, after_ref, keep_ref, send_ref):
    n = keep_ref.shape[0]

    def total(r):
        at = pl.ds(pl.multiple_of(r * n, n), n)
        out = x_ref[0, at, :].astype(f32)
        for i in range(1, x_ref.shape[0]):
            out = out + x_ref[i, at, :].astype(f32)
        return out

    keep_ref[...] = total(rep[0])
    send_ref[...] = total(1 - rep[0]).astype(bf16)


def sum_sides(rep, x, after):
    n = x.shape[1] // 2
    return pl.pallas_call(
        sum_kernel,
        out_shape=(
            jax.ShapeDtypeStruct((n, LANES), f32),
            jax.ShapeDtypeStruct((n, LANES), bf16),
        ),
        in_specs=[smem(), pl.BlockSpec(memory_space=pltpu.VMEM), hbm()],
        compiler_params=pltpu.CompilerParams(vmem_limit_bytes=VMEM),
        name="sum_sides",
    )(rep, x, after)


def across(x, n):
    part = n // 8
    rest = x[3 * n : 3 * n + part].T
    rest = jnp.concatenate([rest[k * REST : (k + 1) * REST] for k in range(8)], axis=1)
    return jnp.concatenate([x[:n].T, x[n : 2 * n].T, x[2 * n : 3 * n].T, rest], axis=0)


def update_kernel(a_ref, b_ref, emb_ref, out_ref):
    width, n = emb_ref.shape
    g = a_ref[...] + b_ref[...].astype(f32)
    new = (emb_ref[...].astype(f32) - 0.5 * across(g, n)).astype(bf16)
    for i in range(n // LANES):
        out_ref[i * width : (i + 1) * width, :] = new[:, i * LANES : (i + 1) * LANES]


def update(a, b, emb):
    width, n = emb.shape
    return pl.pallas_call(
        update_kernel,
        out_shape=jax.ShapeDtypeStruct((width * n // LANES, LANES), bf16),
        compiler_params=pltpu.CompilerParams(vmem_limit_bytes=VMEM),
        name="update",
    )(a, b, emb)


def finish_kernel(place, a_ref, ar_ref, b0_ref, b1_ref, b2_ref, b3_ref, dirty_ref, up_ref, check_ref):
    width = up_ref.shape[0]
    half = dirty_ref.shape[1] // PIECES // 2
    blocks = [(a_ref, k, k, 0) for k in range(4)] + [(ar_ref, k, 4 + k, 0) for k in range(4)]
    for k, ref in enumerate((b0_ref, b1_ref, b2_ref, b3_ref)):
        blocks += [(ref, 0, k, half), (ref, 1, 4 + k, half)]
    for ref, i, at_place, off in blocks:
        start = pl.multiple_of(place[at_place] * 2 * half + off, half)
        for k in range(half // LANES):
            at = pl.ds(pl.multiple_of(start + k * LANES, LANES), LANES)
            x = ref[i, k * width : (k + 1) * width, :]
            up_ref[:, at] = x
            check_ref[:, at] = jnp.where(dirty_ref[:, at] == 1, x.astype(f32), 0.0).astype(bf16)


def finish(place, parts, dirty, width):
    out = jax.ShapeDtypeStruct((width, dirty.shape[1]), bf16)
    return pl.pallas_call(
        finish_kernel,
        in_specs=[smem()] + [pl.BlockSpec(memory_space=pltpu.VMEM)] * 7,
        out_shape=(out, out),
        compiler_params=pltpu.CompilerParams(vmem_limit_bytes=VMEM),
        name="finish",
    )(place, *parts, dirty)


def relation_kernel(m, order, x_ref, out_ref):
    cols = jnp.concatenate(
        [across(x_ref[order[i]].astype(f32), m) for i in range(PIECES)], axis=1
    )
    out_ref[...] = cols[:, : out_ref.shape[1]]


def relation_out(order, x, m, shape):
    return pl.pallas_call(
        functools.partial(relation_kernel, m),
        out_shape=jax.ShapeDtypeStruct(shape, f32),
        in_specs=[smem(), pl.BlockSpec(memory_space=pltpu.VMEM)],
        compiler_params=pltpu.CompilerParams(vmem_limit_bytes=VMEM),
        name="relation_out",
    )(order, x)


def by_side(x):
    sides = lax.axis_size("side")
    return lax.all_to_all(x.reshape(sides, -1, LANES), "side", 0, 0, tiled=True)


def around(x):
    return [x] + [shifted(x, "side", by) for by in (1, -1, 2)]


def both_reps(x):
    return [x, shifted(x, "rep", 1)]


def swapped(x, axis, bit):
    count = lax.axis_size(axis)
    return lax.ppermute(x, axis, [(i, i ^ bit) for i in range(count)])


def local(
    embeddings, relation, source_ids, relation_ids, target_ids, negative_ids, edge_counts, dirty
):
    rows, width = embeddings.shape
    nrel = relation.shape[0]
    doms = lax.axis_size("dom")
    count = edge_counts.reshape(1)
    nneg = negative_ids.shape[-1]
    src = source_ids.reshape(-1) * GROUPS
    rid = relation_ids.reshape(-1) * GROUPS
    dst = target_ids.reshape(-1) * GROUPS
    neg = (jnp.pad(negative_ids[0, 0, 0], ((0, 0), (0, SPAN - nneg))) * GROUPS).reshape(-1)
    me = lax.axis_index("side") * lax.axis_size("rep") + lax.axis_index("rep")
    piece = rows // PIECES
    half = piece // 2
    own = [lax.dynamic_slice_in_dim(embeddings.T, me * piece + h * half, half, 1) for h in (0, 1)]
    side, rep = lax.axis_index("side"), lax.axis_index("rep")
    sides = jnp.stack([side, (side + 3) % 4, (side + 1) % 4, (side + 2) % 4])
    place = jnp.concatenate([sides * 2 + rep, sides * 2 + 1 - rep]).astype(jnp.int32)
    order = jnp.argsort(place).astype(jnp.int32)

    dst_slab = shifted(embeddings, "dom", -1)
    e_rows, r_rows = edge_rows(count, src, rid, embeddings, relation)
    *gdst, grel, values = edge_blocks(nneg, count, rid, dst, neg, dst_slab, e_rows, r_rows, nrel)
    returned = [shifted(g, "dom", 1) for g in gdst]
    which = rep.reshape(1).astype(jnp.int32)
    rel = by_side(grel)
    gsrc = source_rows(count, src, values, rows)
    rel, sent = sum_sides(which, rel, gsrc[0])
    rel = rel + shifted(sent, "rep", 1).astype(f32)
    bit = 1
    while bit < doms:
        rel = rel + swapped(rel, "dom", bit)
        bit *= 2
    rel = jnp.concatenate(around(jnp.stack(both_reps(rel.astype(bf16)))))
    relm = -(-nrel // (PIECES * 64)) * 64
    rel_order = (order % 4) * 2 + order // 4
    relation_grad = relation_out(rel_order, rel, relm, (width, nrel))

    mine = []
    for h in (0, 1):
        keep, sent = sum_sides(which, by_side(gsrc[h] + returned[h]), own[h])
        mine.append(update(keep, shifted(sent, "rep", 1), own[h]))
    a4 = jnp.stack(around(mine[0]))
    parts = both_reps(a4) + around(jnp.stack(both_reps(mine[1])))
    updated, checkpoint = finish(place, parts, dirty[None, :], width)
    return (updated.T, relation_grad.T, checkpoint.T)


def solution(mesh):
    placed = (
        P("dom", None),
        P(),
        P("dom", "side", "rep", None),
        P("dom", "side", "rep", None),
        P("dom", "side", "rep", None),
        P("dom", "side", "rep", None, None),
        P("dom", "side", "rep"),
        P("dom"),
    )
    return jax.shard_map(
        local,
        mesh=mesh,
        in_specs=placed,
        out_specs=(P("dom", None), P(), P("dom", None)),
        check_vma=False,
    )
```

```python
import functools

import jax
import jax.numpy as jnp
from jax import lax
from jax.experimental import pallas as pl
from jax.experimental.pallas import tpu as pltpu
from jax.sharding import PartitionSpec as P

SPAN = 1024
LANES = 128
GROUPS = 4
REST = 16
FLAT = SPAN * GROUPS
CHUNK = SPAN // 2
HALF = FLAT // 2
PIECES = 8
INE = 512
INN = 256
NCOPY = 3
SLOTS = 4
VMEM = 61 * 2**20

f32 = jnp.float32
bf16 = jnp.bfloat16


def shifted(x, axis, by):
    count = lax.axis_size(axis)
    return lax.ppermute(x, axis, [(i, (i + by) % count) for i in range(count)])


def row_of(index):
    return pl.ds(pl.multiple_of(index, GROUPS), GROUPS)


def slot_of(base, k):
    return pl.ds(base + (k // 8) * 8 * GROUPS + k % 8, GROUPS, stride=8)


def tiles(x):
    n = x.shape[0] // GROUPS
    x = x.reshape(n // 8, GROUPS, 8, LANES)
    return [x[:, c].reshape(n, LANES) for c in range(GROUPS)]


def untiles(cols):
    n = cols[0].shape[0]
    x = jnp.concatenate([c.reshape(n // 8, 1, 8, LANES) for c in cols], axis=1)
    return x.reshape(n * GROUPS, LANES)


def gather_rows(ops, base, n):
    for k0 in range(0, n, 8):
        ks = range(k0, k0 + 8)
        held = [[table[row_of(ids[j + k]), :] for table, ids, j, _ in ops] for k in ks]
        for k, rows in zip(ks, held):
            for (_, _, _, out), x in zip(ops, rows):
                out[slot_of(base, k), :] = x


def fill_rows(x, table, first, n):
    x = x.astype(f32)
    for c in range(GROUPS):
        part = x[:, c * LANES : min((c + 1) * LANES, x.shape[1])]
        if part.shape[1] < LANES:
            part = jnp.concatenate(
                [part, jnp.zeros((n, LANES - part.shape[1]), f32)], axis=1
            )
        table[pl.ds(first * GROUPS + c, n, stride=GROUPS), :] = part


def load_table(src_hbm, raw, sems, table):
    part = raw.shape[1]
    count = src_hbm.shape[0] // part

    def copy(i, slot):
        return pltpu.make_async_copy(
            src_hbm.at[pl.ds(pl.multiple_of(i * part, part), part)], raw.at[slot], sems.at[slot]
        )

    for i in range(2):
        copy(i, i).start()

    @pl.loop(0, count)
    def _(i):
        slot = lax.rem(i, 2)
        copy(i, slot).wait()

        @pl.loop(0, part // 64)
        def _(q):
            at = pl.multiple_of(q * 64, 64)
            fill_rows(raw[slot, pl.ds(at, 64), :], table, i * part + at, 64)

        @pl.when(i + 2 < count)
        def _():
            copy(i + 2, slot).start()


def edge_rows_kernel(
    count, src_i, rid_i, emb_hbm, rel_ref, e_out, r_out, ts, tr, raw, eb0, eb1, rb0, rb1, lsem, sems
):
    load_table(emb_hbm, raw, lsem, ts)
    nrel = rel_ref.shape[0]
    whole = nrel // 64

    @pl.loop(0, whole)
    def _(q):
        first = pl.multiple_of(q * 64, 64)
        fill_rows(rel_ref[pl.ds(first, 64), :], tr, first, 64)

    for i in range(whole * 64, nrel):
        fill_rows(rel_ref[i : i + 1, :], tr, i, 1)

    nblocks = (count[0] + SPAN - 1) // SPAN
    outs = ((eb0, e_out, 0), (eb1, e_out, 1), (rb0, r_out, 0), (rb1, r_out, 1))

    def copies(blk, slot):
        return [
            pltpu.make_async_copy(
                buf.at[slot], out.at[blk, pl.ds(h * HALF, HALF)], sems.at[slot, i]
            )
            for i, (buf, out, h) in enumerate(outs)
        ]

    def step(blk, _):
        slot = lax.rem(blk, 2)

        @pl.when(blk >= 2)
        def _():
            for c in copies(blk - 2, slot):
                c.wait()

        e0, e1, r0, r1 = (x.at[slot] for x in (eb0, eb1, rb0, rb1))

        @pl.loop(0, SPAN // 32)
        def _(q):
            base = pl.multiple_of(q * 16 * GROUPS, 64)
            j = blk * SPAN + q * 16
            gather_rows(
                [
                    (ts, src_i, j, e0),
                    (ts, src_i, j + SPAN // 2, e1),
                    (tr, rid_i, j, r0),
                    (tr, rid_i, j + SPAN // 2, r1),
                ],
                base,
                16,
            )

        for c in copies(blk, slot):
            c.start()
        return 0

    lax.fori_loop(0, nblocks, step, 0)

    @pl.when(nblocks >= 2)
    def _():
        for c in copies(nblocks - 2, lax.rem(nblocks, 2)):
            c.wait()

    for c in copies(nblocks - 1, lax.rem(nblocks + 1, 2)):
        c.wait()


def write_piece(first, n, load, stage):
    for c in range(GROUPS - 1):
        stage[c * n : (c + 1) * n, :] = load(c, first, n).astype(stage.dtype)
    part = n // 8
    rest = load(GROUPS - 1, first, part)
    for k in range(1, 8):
        rest = rest + pltpu.roll(load(GROUPS - 1, first + k * part, part), k * REST, 1)
    stage[3 * n : 3 * n + part, :] = rest.astype(stage.dtype)


def zero(acc):
    n = acc.shape[0]
    whole = n // 256

    @pl.loop(0, whole)
    def _(q):
        acc[pl.ds(pl.multiple_of(q * 256, 256), 256), :] = jnp.zeros((256, LANES), f32)

    if n % 256:
        acc[whole * 256 :, :] = jnp.zeros((n - whole * 256, LANES), f32)


def add_rows(ops):
    values = [val[at, :] for _, _, val, at in ops]
    held = [acc[row, :] for acc, row, _, _ in ops]
    for (acc, row, _, _), v, h in zip(ops, values, held):
        acc[row, :] = h + v


def plane(accs):
    def load(c, first, n):
        at = pl.ds(first * GROUPS + c, n, stride=GROUPS)
        x = accs[0][at, :]
        for acc in accs[1:]:
            x = x + acc[at, :]
        return x

    return load


def block_kernel(
    nneg, count, rid_i, dst_i, neg_i, dst_hbm, e_hbm, r_hbm,
    lo_out, hi_out, rel_out, v_out,
    td, a0, a1, a2, r0_acc, r1_acc, raw, eb, rb, db0, db1, nb0, nb1, lb, nbb, dn, stage, rstage, lsem, sems, vsem, osem,
):
    total = count[0]
    nblocks = (total + SPAN - 1) // SPAN

    def fetches(blk, slot):
        return (
            pltpu.make_async_copy(e_hbm.at[blk], eb.at[slot], sems.at[slot, 0]),
            pltpu.make_async_copy(r_hbm.at[blk], rb.at[slot], sems.at[slot, 1]),
        )

    def put(blk, slot):
        return pltpu.make_async_copy(rb.at[slot], v_out.at[blk], vsem.at[slot])

    for c in fetches(0, 0):
        c.start()
    load_table(dst_hbm, raw, lsem, td)
    for acc in (a0, a1, a2, r0_acc, r1_acc):
        zero(acc)

    def step(blk, _):
        slot = lax.rem(blk, 2)

        @pl.when(blk >= 1)
        def _():
            put(blk - 1, 1 - slot).wait()

        @pl.when(blk + 1 < nblocks)
        def _():
            for c in fetches(blk + 1, 1 - slot):
                c.start()

        first = blk * SPAN
        es, rs = eb.at[slot], rb.at[slot]

        @pl.loop(0, SPAN // 32)
        def _(q):
            base = pl.multiple_of(q * 16 * GROUPS, 64)
            j = first + q * 16
            gather_rows(
                [
                    (td, dst_i, j, db0),
                    (td, dst_i, j + CHUNK, db1),
                    (td, neg_i, j, nb0),
                    (td, neg_i, j + CHUNK, nb1),
                ],
                base,
                16,
            )

        for ch, nb in enumerate((nb0, nb1)):
            cols = tiles(nb[...])
            for c in range(GROUPS):
                nbb[ch * CHUNK : (ch + 1) * CHUNK, c * LANES : (c + 1) * LANES] = cols[c].astype(bf16)

        for c in fetches(blk, slot):
            c.wait()

        def dense(ch, db):
            r0 = ch * CHUNK
            flat = pl.ds(ch * HALF, HALF)
            e = tiles(es[flat, :])
            r = tiles(rs[flat, :])
            d = tiles(db[...])
            left = [(e[c] * r[c]).astype(bf16) for c in range(GROUPS)]
            leftf = [x.astype(f32) for x in left]
            prod = leftf[0] * d[0]
            for c in range(1, GROUPS):
                prod = prod + leftf[c] * d[c]
            positive = jnp.sum(prod, axis=1, keepdims=True)
            lc = jnp.concatenate(left, axis=1)
            lb[pl.ds(r0, CHUNK), :] = lc
            negative = lax.dot_general(
                lc, nbb[...], (((1,), (1,)), ((), ())), preferred_element_type=f32
            )
            edge = nneg // LANES * LANES
            lane = lax.broadcasted_iota(jnp.int32, (CHUNK, SPAN - edge), 1)
            negative = jnp.concatenate(
                [negative[:, :edge], jnp.where(lane < nneg - edge, negative[:, edge:], -jnp.inf)], axis=1
            )
            top = jnp.maximum(positive, jnp.max(negative, axis=1, keepdims=True))
            e_pos = jnp.exp(positive - top)
            e_neg = jnp.exp(negative - top)
            z = e_pos + jnp.sum(e_neg, axis=1, keepdims=True)
            row = lax.broadcasted_iota(jnp.int32, (CHUNK, 1), 0) + (first + r0)
            live = jnp.where(row < total, 1.0, 0.0).astype(f32)
            inv = 1.0 / z
            d_pos = live * (e_pos * inv - 1.0)
            d_neg = (e_neg * (live * inv)).astype(bf16)
            dn[pl.ds(r0, CHUNK), :] = d_neg
            dl = jnp.dot(d_neg, nbb[...], preferred_element_type=f32)
            x = [d_pos * d[c] + dl[:, c * LANES : (c + 1) * LANES] for c in range(GROUPS)]
            db[...] = untiles([d_pos * leftf[c] for c in range(GROUPS)])
            es[flat, :] = untiles([x[c] * e[c] for c in range(GROUPS)])
            rs[flat, :] = untiles([x[c] * r[c] for c in range(GROUPS)])


        def negative_rows(ch, nb):
            part = lax.dot_general(
                dn[:, ch * CHUNK : (ch + 1) * CHUNK], lb[...], (((0,), (0,)), ((), ())),
                preferred_element_type=f32,
            )
            nb[...] = untiles([part[:, c * LANES : (c + 1) * LANES] for c in range(GROUPS)])

        def add_edges(h, start, base, n):
            db, ev = (db0, db1)[h], es.at[pl.ds(h * HALF, HALF)]
            j0 = first + h * CHUNK + start
            for t in range(0, n, 2):
                ops = []
                for i in range(2):
                    k, at = t + i, slot_of(base, t + i)
                    ops.append(((a0, a1)[i], row_of(dst_i[j0 + k]), db, at))
                    ops.append(((r0_acc, r1_acc)[i], row_of(rid_i[j0 + k]), ev, at))
                add_rows(ops)

        def add_negatives(h, start, base, n):
            nb = (nb0, nb1)[h]
            j0 = first + h * CHUNK + start
            for t in range(0, n, NCOPY):
                add_rows(
                    [
                        ((a0, a1, a2)[i], row_of(neg_i[j0 + t + i]), nb, slot_of(base, t + i))
                        for i in range(min(NCOPY, n - t))
                    ]
                )

        def looped(step, h, start, stop):
            @pl.loop(0, (stop - start) // 16)
            def _(q):
                at = pl.multiple_of(start + q * 16, 16)
                step(h, at, pl.multiple_of(at * GROUPS, 64), 16)

        dense(0, db0)
        add_edges(0, 0, 0, CHUNK)
        dense(1, db1)
        put(blk, slot).start()
        add_edges(1, 0, 0, INE)
        negative_rows(0, nb0)
        add_negatives(0, 0, 0, INN)
        negative_rows(1, nb1)
        if INE < CHUNK:
            looped(add_edges, 1, INE, CHUNK)
        if INN < CHUNK:
            looped(add_negatives, 0, INN, CHUNK)
        looped(add_negatives, 1, 0, CHUNK)
        return 0

    lax.fori_loop(0, nblocks, step, 0)
    last = nblocks - 1
    put(last, lax.rem(last, 2)).wait()

    m = r0_acc.shape[0] // GROUPS // PIECES
    packed = m * 25 // 8
    grad, rel = plane((a0, a1, a2)), plane((r0_acc, r1_acc))

    def fill_rel(j, st):
        write_piece(j * m, m, rel, st)
        if st.shape[0] > packed:
            st[packed:, :] = jnp.zeros((st.shape[0] - packed, LANES), st.dtype)

    emit_halves(grad, td.shape[0] // GROUPS, lo_out, hi_out, stage, osem)
    emit(fill_rel, rel_out, rstage, osem)


def emit(fill, out, stage, sem):
    def copy(j, slot):
        return pltpu.make_async_copy(stage.at[slot], out.at[j], sem.at[slot])

    @pl.loop(0, PIECES)
    def _(j):
        slot = lax.rem(j, SLOTS)

        @pl.when(j >= SLOTS)
        def _():
            copy(j - SLOTS, slot).wait()

        fill(j, stage.at[slot])
        copy(j, slot).start()

    for j in range(PIECES - SLOTS, PIECES):
        copy(j, j % SLOTS).wait()


def emit_halves(load, rows, lo_out, hi_out, stage, sem):
    half = rows // PIECES // 2
    for h, out in enumerate((lo_out, hi_out)):
        emit(
            lambda j, st, h=h: write_piece((2 * j + h) * half, half, load, st), out, stage, sem
        )


def source_kernel(count, src_i, v_hbm, lo_out, hi_out, a0, a1, a2, a3, vb, stage, sems, osem):
    nblocks = (count[0] + SPAN - 1) // SPAN
    accs = (a0, a1, a2, a3)

    def fetch(blk, slot):
        return pltpu.make_async_copy(v_hbm.at[blk], vb.at[slot], sems.at[slot])

    fetch(0, 0).start()
    for acc in accs:
        zero(acc)

    def step(blk, _):
        slot = lax.rem(blk, 2)

        @pl.when(blk + 1 < nblocks)
        def _():
            fetch(blk + 1, 1 - slot).start()

        fetch(blk, slot).wait()
        vs = vb.at[slot]

        @pl.loop(0, SPAN // 16)
        def _(q):
            base = pl.multiple_of(q * 16 * GROUPS, 64)
            for t in range(0, 16, 4):
                add_rows(
                    [
                        (accs[i], row_of(src_i[blk * SPAN + q * 16 + t + i]), vs, slot_of(base, t + i))
                        for i in range(4)
                    ]
                )

        return 0

    lax.fori_loop(0, nblocks, step, 0)
    emit_halves(plane(accs), a0.shape[0] // GROUPS, lo_out, hi_out, stage, osem)


def smem():
    return pl.BlockSpec(memory_space=pltpu.SMEM)


def hbm():
    return pl.BlockSpec(memory_space=pl.ANY)


def edge_rows(count, src, rid, emb, relation):
    nb = src.shape[0] // SPAN
    rows = emb.shape[0]
    nrel = relation.shape[0]
    shape = jax.ShapeDtypeStruct((nb, FLAT, LANES), f32)
    return pl.pallas_call(
        edge_rows_kernel,
        out_shape=(shape, shape),
        in_specs=[smem()] * 3 + [hbm(), pl.BlockSpec(memory_space=pltpu.VMEM)],
        out_specs=(hbm(), hbm()),
        scratch_shapes=[
            pltpu.VMEM((rows * GROUPS, LANES), f32),
            pltpu.VMEM((-(-nrel // 8) * 8 * GROUPS, LANES), f32),
            pltpu.VMEM((2, 512, emb.shape[1]), bf16),
            pltpu.VMEM((2, HALF, LANES), f32),
            pltpu.VMEM((2, HALF, LANES), f32),
            pltpu.VMEM((2, HALF, LANES), f32),
            pltpu.VMEM((2, HALF, LANES), f32),
            pltpu.SemaphoreType.DMA((2,)),
            pltpu.SemaphoreType.DMA((2, 4)),
        ],
        compiler_params=pltpu.CompilerParams(vmem_limit_bytes=VMEM),
        cost_estimate=pl.CostEstimate(flops=0, bytes_accessed=60_000_000, transcendentals=0),
        name="edge_rows",
    )(count, src, rid, emb, relation)


def edge_blocks(nneg, count, rid, dst, neg, dst_slab, e_rows, r_rows, nrel):
    rows = dst_slab.shape[0]
    packed = rows // PIECES // 2 * 25 // 8
    half = jax.ShapeDtypeStruct((PIECES, packed, LANES), bf16)
    relm = -(-nrel // (PIECES * 64)) * 64
    relrows = -(-(relm * 25 // 8) // 128) * 128
    table = pltpu.VMEM((rows * GROUPS, LANES), f32)
    rel = pltpu.VMEM((relm * PIECES * GROUPS, LANES), f32)
    return pl.pallas_call(
        functools.partial(block_kernel, nneg),
        out_shape=(
            half,
            half,
            jax.ShapeDtypeStruct((PIECES, relrows, LANES), bf16),
            jax.ShapeDtypeStruct(r_rows.shape, f32),
        ),
        in_specs=[smem()] * 4 + [hbm()] * 3,
        out_specs=(hbm(), hbm(), hbm(), hbm()),
        scratch_shapes=[
            table, table, table, table, rel, rel,
            pltpu.VMEM((2, 512, dst_slab.shape[1]), bf16),
            pltpu.VMEM((2, FLAT, LANES), f32),
            pltpu.VMEM((2, FLAT, LANES), f32),
            pltpu.VMEM((HALF, LANES), f32),
            pltpu.VMEM((HALF, LANES), f32),
            pltpu.VMEM((HALF, LANES), f32),
            pltpu.VMEM((HALF, LANES), f32),
            pltpu.VMEM((SPAN, LANES * GROUPS), bf16),
            pltpu.VMEM((SPAN, LANES * GROUPS), bf16),
            pltpu.VMEM((SPAN, SPAN), bf16),
            pltpu.VMEM((SLOTS, packed, LANES), bf16),
            pltpu.VMEM((SLOTS, relrows, LANES), bf16),
            pltpu.SemaphoreType.DMA((2,)),
            pltpu.SemaphoreType.DMA((2, 2)),
            pltpu.SemaphoreType.DMA((2,)),
            pltpu.SemaphoreType.DMA((SLOTS,)),
        ],
        compiler_params=pltpu.CompilerParams(vmem_limit_bytes=VMEM),
        name="edge_blocks",
    )(count, rid, dst, neg, dst_slab, e_rows, r_rows)


def source_rows(count, src, values, rows):
    packed = rows // PIECES // 2 * 25 // 8
    half = jax.ShapeDtypeStruct((PIECES, packed, LANES), bf16)
    table = pltpu.VMEM((rows * GROUPS, LANES), f32)
    return pl.pallas_call(
        source_kernel,
        out_shape=(half, half),
        in_specs=[smem()] * 2 + [hbm()],
        out_specs=(hbm(), hbm()),
        scratch_shapes=[
            table, table, table, table,
            pltpu.VMEM((2, FLAT, LANES), f32),
            pltpu.VMEM((SLOTS, packed, LANES), bf16),
            pltpu.SemaphoreType.DMA((2,)),
            pltpu.SemaphoreType.DMA((SLOTS,)),
        ],
        compiler_params=pltpu.CompilerParams(vmem_limit_bytes=VMEM),
        cost_estimate=pl.CostEstimate(flops=0, bytes_accessed=60_000_000, transcendentals=0),
        name="source_rows",
    )(count, src, values)


def sum_kernel(rep, x_ref, after_ref, keep_ref, send_ref):
    n = keep_ref.shape[0]

    def total(r):
        at = pl.ds(pl.multiple_of(r * n, n), n)
        out = x_ref[0, at, :].astype(f32)
        for i in range(1, x_ref.shape[0]):
            out = out + x_ref[i, at, :].astype(f32)
        return out

    keep_ref[...] = total(rep[0])
    send_ref[...] = total(1 - rep[0]).astype(bf16)


def sum_sides(rep, x, after):
    n = x.shape[1] // 2
    return pl.pallas_call(
        sum_kernel,
        out_shape=(
            jax.ShapeDtypeStruct((n, LANES), f32),
            jax.ShapeDtypeStruct((n, LANES), bf16),
        ),
        in_specs=[smem(), pl.BlockSpec(memory_space=pltpu.VMEM), hbm()],
        compiler_params=pltpu.CompilerParams(vmem_limit_bytes=VMEM),
        name="sum_sides",
    )(rep, x, after)


def across(x, n):
    part = n // 8
    rest = x[3 * n : 3 * n + part].T
    rest = jnp.concatenate([rest[k * REST : (k + 1) * REST] for k in range(8)], axis=1)
    return jnp.concatenate([x[:n].T, x[n : 2 * n].T, x[2 * n : 3 * n].T, rest], axis=0)


def update_kernel(a_ref, b_ref, emb_ref, out_ref):
    width, n = emb_ref.shape
    g = a_ref[...] + b_ref[...].astype(f32)
    new = (emb_ref[...].astype(f32) - 0.5 * across(g, n)).astype(bf16)
    for i in range(n // LANES):
        out_ref[i * width : (i + 1) * width, :] = new[:, i * LANES : (i + 1) * LANES]


def update(a, b, emb):
    width, n = emb.shape
    return pl.pallas_call(
        update_kernel,
        out_shape=jax.ShapeDtypeStruct((width * n // LANES, LANES), bf16),
        compiler_params=pltpu.CompilerParams(vmem_limit_bytes=VMEM),
        name="update",
    )(a, b, emb)


def finish_kernel(place, a_ref, ar_ref, b0_ref, b1_ref, b2_ref, b3_ref, dirty_ref, up_ref, check_ref):
    width = up_ref.shape[0]
    half = dirty_ref.shape[1] // PIECES // 2
    blocks = [(a_ref, k, k, 0) for k in range(4)] + [(ar_ref, k, 4 + k, 0) for k in range(4)]
    for k, ref in enumerate((b0_ref, b1_ref, b2_ref, b3_ref)):
        blocks += [(ref, 0, k, half), (ref, 1, 4 + k, half)]
    for ref, i, at_place, off in blocks:
        start = pl.multiple_of(place[at_place] * 2 * half + off, half)
        for k in range(half // LANES):
            at = pl.ds(pl.multiple_of(start + k * LANES, LANES), LANES)
            x = ref[i, k * width : (k + 1) * width, :]
            up_ref[:, at] = x
            check_ref[:, at] = jnp.where(dirty_ref[:, at] == 1, x.astype(f32), 0.0).astype(bf16)


def finish(place, parts, dirty, width):
    out = jax.ShapeDtypeStruct((width, dirty.shape[1]), bf16)
    return pl.pallas_call(
        finish_kernel,
        in_specs=[smem()] + [pl.BlockSpec(memory_space=pltpu.VMEM)] * 7,
        out_shape=(out, out),
        compiler_params=pltpu.CompilerParams(vmem_limit_bytes=VMEM),
        name="finish",
    )(place, *parts, dirty)


def relation_kernel(m, order, x_ref, out_ref):
    cols = jnp.concatenate(
        [across(x_ref[order[i]].astype(f32), m) for i in range(PIECES)], axis=1
    )
    out_ref[...] = cols[:, : out_ref.shape[1]]


def relation_out(order, x, m, shape):
    return pl.pallas_call(
        functools.partial(relation_kernel, m),
        out_shape=jax.ShapeDtypeStruct(shape, f32),
        in_specs=[smem(), pl.BlockSpec(memory_space=pltpu.VMEM)],
        compiler_params=pltpu.CompilerParams(vmem_limit_bytes=VMEM),
        name="relation_out",
    )(order, x)


def by_side(x):
    sides = lax.axis_size("side")
    return lax.all_to_all(x.reshape(sides, -1, LANES), "side", 0, 0, tiled=True)


def around(x):
    return [x] + [shifted(x, "side", by) for by in (1, -1, 2)]


def both_reps(x):
    return [x, shifted(x, "rep", 1)]


def swapped(x, axis, bit):
    count = lax.axis_size(axis)
    return lax.ppermute(x, axis, [(i, i ^ bit) for i in range(count)])


def local(
    embeddings, relation, source_ids, relation_ids, target_ids, negative_ids, edge_counts, dirty
):
    rows, width = embeddings.shape
    nrel = relation.shape[0]
    doms = lax.axis_size("dom")
    count = edge_counts.reshape(1)
    nneg = negative_ids.shape[-1]
    src = source_ids.reshape(-1) * GROUPS
    rid = relation_ids.reshape(-1) * GROUPS
    dst = target_ids.reshape(-1) * GROUPS
    neg = (jnp.pad(negative_ids[0, 0, 0], ((0, 0), (0, SPAN - nneg))) * GROUPS).reshape(-1)
    me = lax.axis_index("side") * lax.axis_size("rep") + lax.axis_index("rep")
    piece = rows // PIECES
    half = piece // 2
    own = [lax.dynamic_slice_in_dim(embeddings.T, me * piece + h * half, half, 1) for h in (0, 1)]
    side, rep = lax.axis_index("side"), lax.axis_index("rep")
    sides = jnp.stack([side, (side + 3) % 4, (side + 1) % 4, (side + 2) % 4])
    place = jnp.concatenate([sides * 2 + rep, sides * 2 + 1 - rep]).astype(jnp.int32)
    order = jnp.argsort(place).astype(jnp.int32)

    dst_slab = shifted(embeddings, "dom", -1)
    e_rows, r_rows = edge_rows(count, src, rid, embeddings, relation)
    *gdst, grel, values = edge_blocks(nneg, count, rid, dst, neg, dst_slab, e_rows, r_rows, nrel)
    returned = [shifted(g, "dom", 1) for g in gdst]
    which = rep.reshape(1).astype(jnp.int32)
    rel = by_side(grel)
    gsrc = source_rows(count, src, values, rows)
    rel, sent = sum_sides(which, rel, gsrc[0])
    rel = rel + shifted(sent, "rep", 1).astype(f32)
    bit = 1
    while bit < doms:
        rel = rel + swapped(rel, "dom", bit)
        bit *= 2
    rel = jnp.concatenate(around(jnp.stack(both_reps(rel.astype(bf16)))))
    relm = -(-nrel // (PIECES * 64)) * 64
    rel_order = (order % 4) * 2 + order // 4
    relation_grad = relation_out(rel_order, rel, relm, (width, nrel))

    mine = []
    for h in (0, 1):
        keep, sent = sum_sides(which, by_side(gsrc[h] + returned[h]), own[h])
        mine.append(update(keep, shifted(sent, "rep", 1), own[h]))
    a4 = jnp.stack(around(mine[0]))
    parts = both_reps(a4) + around(jnp.stack(both_reps(mine[1])))
    updated, checkpoint = finish(place, parts, dirty[None, :], width)
    return (updated.T, relation_grad.T, checkpoint.T)


def solution(mesh):
    placed = (
        P("dom", None),
        P(),
        P("dom", "side", "rep", None),
        P("dom", "side", "rep", None),
        P("dom", "side", "rep", None),
        P("dom", "side", "rep", None, None),
        P("dom", "side", "rep"),
        P("dom"),
    )
    return jax.shard_map(
        local,
        mesh=mesh,
        in_specs=placed,
        out_specs=(P("dom", None), P(), P("dom", None)),
        check_vma=False,
    )
```

```python
import functools

import jax
import jax.numpy as jnp
from jax import lax
from jax.experimental import pallas as pl
from jax.experimental.pallas import tpu as pltpu
from jax.sharding import PartitionSpec as P

SPAN = 1024
LANES = 128
GROUPS = 4
REST = 16
FLAT = SPAN * GROUPS
CHUNK = SPAN // 2
HALF = FLAT // 2
PIECES = 8
INE = 512
INN = 256
NCOPY = 3
SLOTS = 4
VMEM = 61 * 2**20

f32 = jnp.float32
bf16 = jnp.bfloat16


def shifted(x, axis, by):
    count = lax.axis_size(axis)
    return lax.ppermute(x, axis, [(i, (i + by) % count) for i in range(count)])


def row_of(index):
    return pl.ds(pl.multiple_of(index, GROUPS), GROUPS)


def slot_of(base, k):
    return pl.ds(base + (k // 8) * 8 * GROUPS + k % 8, GROUPS, stride=8)


def tiles(x):
    n = x.shape[0] // GROUPS
    x = x.reshape(n // 8, GROUPS, 8, LANES)
    return [x[:, c].reshape(n, LANES) for c in range(GROUPS)]


def untiles(cols):
    n = cols[0].shape[0]
    x = jnp.concatenate([c.reshape(n // 8, 1, 8, LANES) for c in cols], axis=1)
    return x.reshape(n * GROUPS, LANES)


def gather_rows(ops, base, n):
    for k0 in range(0, n, 8):
        ks = range(k0, k0 + 8)
        held = [[table[row_of(ids[j + k]), :] for table, ids, j, _ in ops] for k in ks]
        for k, rows in zip(ks, held):
            for (_, _, _, out), x in zip(ops, rows):
                out[slot_of(base, k), :] = x


def fill_rows(x, table, first, n):
    x = x.astype(f32)
    for c in range(GROUPS):
        part = x[:, c * LANES : min((c + 1) * LANES, x.shape[1])]
        if part.shape[1] < LANES:
            part = jnp.concatenate(
                [part, jnp.zeros((n, LANES - part.shape[1]), f32)], axis=1
            )
        table[pl.ds(first * GROUPS + c, n, stride=GROUPS), :] = part


def load_table(src_hbm, raw, sems, table):
    part = raw.shape[1]
    count = src_hbm.shape[0] // part

    def copy(i, slot):
        return pltpu.make_async_copy(
            src_hbm.at[pl.ds(pl.multiple_of(i * part, part), part)], raw.at[slot], sems.at[slot]
        )

    for i in range(2):
        copy(i, i).start()

    @pl.loop(0, count)
    def _(i):
        slot = lax.rem(i, 2)
        copy(i, slot).wait()

        @pl.loop(0, part // 64)
        def _(q):
            at = pl.multiple_of(q * 64, 64)
            fill_rows(raw[slot, pl.ds(at, 64), :], table, i * part + at, 64)

        @pl.when(i + 2 < count)
        def _():
            copy(i + 2, slot).start()


def edge_rows_kernel(
    count, src_i, rid_i, emb_hbm, rel_ref, e_out, r_out, ts, tr, raw, eb0, eb1, rb0, rb1, lsem, sems
):
    load_table(emb_hbm, raw, lsem, ts)
    nrel = rel_ref.shape[0]
    whole = nrel // 64

    @pl.loop(0, whole)
    def _(q):
        first = pl.multiple_of(q * 64, 64)
        fill_rows(rel_ref[pl.ds(first, 64), :], tr, first, 64)

    for i in range(whole * 64, nrel):
        fill_rows(rel_ref[i : i + 1, :], tr, i, 1)

    nblocks = (count[0] + SPAN - 1) // SPAN
    outs = ((eb0, e_out, 0), (eb1, e_out, 1), (rb0, r_out, 0), (rb1, r_out, 1))

    def copies(blk, slot):
        return [
            pltpu.make_async_copy(
                buf.at[slot], out.at[blk, pl.ds(h * HALF, HALF)], sems.at[slot, i]
            )
            for i, (buf, out, h) in enumerate(outs)
        ]

    def step(blk, _):
        slot = lax.rem(blk, 2)

        @pl.when(blk >= 2)
        def _():
            for c in copies(blk - 2, slot):
                c.wait()

        e0, e1, r0, r1 = (x.at[slot] for x in (eb0, eb1, rb0, rb1))

        @pl.loop(0, SPAN // 32)
        def _(q):
            base = pl.multiple_of(q * 16 * GROUPS, 64)
            j = blk * SPAN + q * 16
            gather_rows(
                [
                    (ts, src_i, j, e0),
                    (ts, src_i, j + SPAN // 2, e1),
                    (tr, rid_i, j, r0),
                    (tr, rid_i, j + SPAN // 2, r1),
                ],
                base,
                16,
            )

        for c in copies(blk, slot):
            c.start()
        return 0

    lax.fori_loop(0, nblocks, step, 0)

    @pl.when(nblocks >= 2)
    def _():
        for c in copies(nblocks - 2, lax.rem(nblocks, 2)):
            c.wait()

    for c in copies(nblocks - 1, lax.rem(nblocks + 1, 2)):
        c.wait()


def write_piece(first, n, load, stage):
    for c in range(GROUPS - 1):
        stage[c * n : (c + 1) * n, :] = load(c, first, n).astype(stage.dtype)
    part = n // 8
    rest = load(GROUPS - 1, first, part)
    for k in range(1, 8):
        rest = rest + pltpu.roll(load(GROUPS - 1, first + k * part, part), k * REST, 1)
    stage[3 * n : 3 * n + part, :] = rest.astype(stage.dtype)


def zero(acc):
    n = acc.shape[0]
    whole = n // 256

    @pl.loop(0, whole)
    def _(q):
        acc[pl.ds(pl.multiple_of(q * 256, 256), 256), :] = jnp.zeros((256, LANES), f32)

    if n % 256:
        acc[whole * 256 :, :] = jnp.zeros((n - whole * 256, LANES), f32)


def add_rows(ops):
    values = [val[at, :] for _, _, val, at in ops]
    held = [acc[row, :] for acc, row, _, _ in ops]
    for (acc, row, _, _), v, h in zip(ops, values, held):
        acc[row, :] = h + v


def plane(accs):
    def load(c, first, n):
        at = pl.ds(first * GROUPS + c, n, stride=GROUPS)
        x = accs[0][at, :]
        for acc in accs[1:]:
            x = x + acc[at, :]
        return x

    return load


def block_kernel(
    nneg, count, rid_i, dst_i, neg_i, dst_hbm, e_hbm, r_hbm,
    lo_out, hi_out, rel_out, v_out,
    td, a0, a1, a2, r0_acc, r1_acc, raw, eb, rb, db0, db1, nb0, nb1, lb, nbb, dn, stage, rstage, lsem, sems, vsem, osem,
):
    total = count[0]
    nblocks = (total + SPAN - 1) // SPAN

    def fetches(blk, slot):
        return (
            pltpu.make_async_copy(e_hbm.at[blk], eb.at[slot], sems.at[slot, 0]),
            pltpu.make_async_copy(r_hbm.at[blk], rb.at[slot], sems.at[slot, 1]),
        )

    def put(blk, slot):
        return pltpu.make_async_copy(rb.at[slot], v_out.at[blk], vsem.at[slot])

    for c in fetches(0, 0):
        c.start()
    load_table(dst_hbm, raw, lsem, td)
    for acc in (a0, a1, a2, r0_acc, r1_acc):
        zero(acc)

    def step(blk, _):
        slot = lax.rem(blk, 2)

        @pl.when(blk >= 1)
        def _():
            put(blk - 1, 1 - slot).wait()

        @pl.when(blk + 1 < nblocks)
        def _():
            for c in fetches(blk + 1, 1 - slot):
                c.start()

        first = blk * SPAN
        es, rs = eb.at[slot], rb.at[slot]

        @pl.loop(0, SPAN // 32)
        def _(q):
            base = pl.multiple_of(q * 16 * GROUPS, 64)
            j = first + q * 16
            gather_rows(
                [
                    (td, dst_i, j, db0),
                    (td, dst_i, j + CHUNK, db1),
                    (td, neg_i, j, nb0),
                    (td, neg_i, j + CHUNK, nb1),
                ],
                base,
                16,
            )

        for ch, nb in enumerate((nb0, nb1)):
            cols = tiles(nb[...])
            for c in range(GROUPS):
                nbb[ch * CHUNK : (ch + 1) * CHUNK, c * LANES : (c + 1) * LANES] = cols[c].astype(bf16)

        for c in fetches(blk, slot):
            c.wait()

        def dense(ch, db):
            r0 = ch * CHUNK
            flat = pl.ds(ch * HALF, HALF)
            e = tiles(es[flat, :])
            r = tiles(rs[flat, :])
            d = tiles(db[...])
            left = [(e[c] * r[c]).astype(bf16) for c in range(GROUPS)]
            leftf = [x.astype(f32) for x in left]
            prod = leftf[0] * d[0]
            for c in range(1, GROUPS):
                prod = prod + leftf[c] * d[c]
            positive = jnp.sum(prod, axis=1, keepdims=True)
            lc = jnp.concatenate(left, axis=1)
            lb[pl.ds(r0, CHUNK), :] = lc
            negative = lax.dot_general(
                lc, nbb[...], (((1,), (1,)), ((), ())), preferred_element_type=f32
            )
            edge = nneg // LANES * LANES
            lane = lax.broadcasted_iota(jnp.int32, (CHUNK, SPAN - edge), 1)
            negative = jnp.concatenate(
                [negative[:, :edge], jnp.where(lane < nneg - edge, negative[:, edge:], -jnp.inf)], axis=1
            )
            top = jnp.maximum(positive, jnp.max(negative, axis=1, keepdims=True))
            e_pos = jnp.exp(positive - top)
            e_neg = jnp.exp(negative - top)
            z = e_pos + jnp.sum(e_neg, axis=1, keepdims=True)
            row = lax.broadcasted_iota(jnp.int32, (CHUNK, 1), 0) + (first + r0)
            live = jnp.where(row < total, 1.0, 0.0).astype(f32)
            inv = 1.0 / z
            d_pos = live * (e_pos * inv - 1.0)
            d_neg = (e_neg * (live * inv)).astype(bf16)
            dn[pl.ds(r0, CHUNK), :] = d_neg
            dl = jnp.dot(d_neg, nbb[...], preferred_element_type=f32)
            x = [d_pos * d[c] + dl[:, c * LANES : (c + 1) * LANES] for c in range(GROUPS)]
            db[...] = untiles([d_pos * leftf[c] for c in range(GROUPS)])
            es[flat, :] = untiles([x[c] * e[c] for c in range(GROUPS)])
            rs[flat, :] = untiles([x[c] * r[c] for c in range(GROUPS)])


        def negative_rows(ch, nb):
            part = lax.dot_general(
                dn[:, ch * CHUNK : (ch + 1) * CHUNK], lb[...], (((0,), (0,)), ((), ())),
                preferred_element_type=f32,
            )
            nb[...] = untiles([part[:, c * LANES : (c + 1) * LANES] for c in range(GROUPS)])

        def add_edges(h, start, base, n):
            db, ev = (db0, db1)[h], es.at[pl.ds(h * HALF, HALF)]
            j0 = first + h * CHUNK + start
            for t in range(0, n, 2):
                ops = []
                for i in range(2):
                    k, at = t + i, slot_of(base, t + i)
                    ops.append(((a0, a1)[i], row_of(dst_i[j0 + k]), db, at))
                    ops.append(((r0_acc, r1_acc)[i], row_of(rid_i[j0 + k]), ev, at))
                add_rows(ops)

        def add_negatives(h, start, base, n):
            nb = (nb0, nb1)[h]
            j0 = first + h * CHUNK + start
            for t in range(0, n, NCOPY):
                add_rows(
                    [
                        ((a0, a1, a2)[i], row_of(neg_i[j0 + t + i]), nb, slot_of(base, t + i))
                        for i in range(min(NCOPY, n - t))
                    ]
                )

        def looped(step, h, start, stop):
            @pl.loop(0, (stop - start) // 16)
            def _(q):
                at = pl.multiple_of(start + q * 16, 16)
                step(h, at, pl.multiple_of(at * GROUPS, 64), 16)

        dense(0, db0)
        add_edges(0, 0, 0, CHUNK)
        dense(1, db1)
        put(blk, slot).start()
        add_edges(1, 0, 0, INE)
        negative_rows(0, nb0)
        add_negatives(0, 0, 0, INN)
        negative_rows(1, nb1)
        if INE < CHUNK:
            looped(add_edges, 1, INE, CHUNK)
        if INN < CHUNK:
            looped(add_negatives, 0, INN, CHUNK)
        looped(add_negatives, 1, 0, CHUNK)
        return 0

    lax.fori_loop(0, nblocks, step, 0)
    last = nblocks - 1
    put(last, lax.rem(last, 2)).wait()

    m = r0_acc.shape[0] // GROUPS // PIECES
    packed = m * 25 // 8
    grad, rel = plane((a0, a1, a2)), plane((r0_acc, r1_acc))

    def fill_rel(j, st):
        write_piece(j * m, m, rel, st)
        if st.shape[0] > packed:
            st[packed:, :] = jnp.zeros((st.shape[0] - packed, LANES), st.dtype)

    emit_halves(grad, td.shape[0] // GROUPS, lo_out, hi_out, stage, osem)
    emit(fill_rel, rel_out, rstage, osem)


def emit(fill, out, stage, sem):
    def copy(j, slot):
        return pltpu.make_async_copy(stage.at[slot], out.at[j], sem.at[slot])

    @pl.loop(0, PIECES)
    def _(j):
        slot = lax.rem(j, SLOTS)

        @pl.when(j >= SLOTS)
        def _():
            copy(j - SLOTS, slot).wait()

        fill(j, stage.at[slot])
        copy(j, slot).start()

    for j in range(PIECES - SLOTS, PIECES):
        copy(j, j % SLOTS).wait()


def emit_halves(load, rows, lo_out, hi_out, stage, sem):
    half = rows // PIECES // 2
    for h, out in enumerate((lo_out, hi_out)):
        emit(
            lambda j, st, h=h: write_piece((2 * j + h) * half, half, load, st), out, stage, sem
        )


def source_kernel(count, src_i, v_hbm, lo_out, hi_out, a0, a1, a2, a3, vb, stage, sems, osem):
    nblocks = (count[0] + SPAN - 1) // SPAN
    accs = (a0, a1, a2, a3)

    def fetch(blk, slot):
        return pltpu.make_async_copy(v_hbm.at[blk], vb.at[slot], sems.at[slot])

    fetch(0, 0).start()
    for acc in accs:
        zero(acc)

    def step(blk, _):
        slot = lax.rem(blk, 2)

        @pl.when(blk + 1 < nblocks)
        def _():
            fetch(blk + 1, 1 - slot).start()

        fetch(blk, slot).wait()
        vs = vb.at[slot]

        @pl.loop(0, SPAN // 16)
        def _(q):
            base = pl.multiple_of(q * 16 * GROUPS, 64)
            for t in range(0, 16, 4):
                add_rows(
                    [
                        (accs[i], row_of(src_i[blk * SPAN + q * 16 + t + i]), vs, slot_of(base, t + i))
                        for i in range(4)
                    ]
                )

        return 0

    lax.fori_loop(0, nblocks, step, 0)
    emit_halves(plane(accs), a0.shape[0] // GROUPS, lo_out, hi_out, stage, osem)


def smem():
    return pl.BlockSpec(memory_space=pltpu.SMEM)


def hbm():
    return pl.BlockSpec(memory_space=pl.ANY)


def edge_rows(count, src, rid, emb, relation):
    nb = src.shape[0] // SPAN
    rows = emb.shape[0]
    nrel = relation.shape[0]
    shape = jax.ShapeDtypeStruct((nb, FLAT, LANES), f32)
    return pl.pallas_call(
        edge_rows_kernel,
        out_shape=(shape, shape),
        in_specs=[smem()] * 3 + [hbm(), pl.BlockSpec(memory_space=pltpu.VMEM)],
        out_specs=(hbm(), hbm()),
        scratch_shapes=[
            pltpu.VMEM((rows * GROUPS, LANES), f32),
            pltpu.VMEM((-(-nrel // 8) * 8 * GROUPS, LANES), f32),
            pltpu.VMEM((2, 512, emb.shape[1]), bf16),
            pltpu.VMEM((2, HALF, LANES), f32),
            pltpu.VMEM((2, HALF, LANES), f32),
            pltpu.VMEM((2, HALF, LANES), f32),
            pltpu.VMEM((2, HALF, LANES), f32),
            pltpu.SemaphoreType.DMA((2,)),
            pltpu.SemaphoreType.DMA((2, 4)),
        ],
        compiler_params=pltpu.CompilerParams(vmem_limit_bytes=VMEM),
        cost_estimate=pl.CostEstimate(flops=0, bytes_accessed=60_000_000, transcendentals=0),
        name="edge_rows",
    )(count, src, rid, emb, relation)


def edge_blocks(nneg, count, rid, dst, neg, dst_slab, e_rows, r_rows, nrel):
    rows = dst_slab.shape[0]
    packed = rows // PIECES // 2 * 25 // 8
    half = jax.ShapeDtypeStruct((PIECES, packed, LANES), bf16)
    relm = -(-nrel // (PIECES * 64)) * 64
    relrows = -(-(relm * 25 // 8) // 128) * 128
    table = pltpu.VMEM((rows * GROUPS, LANES), f32)
    rel = pltpu.VMEM((relm * PIECES * GROUPS, LANES), f32)
    return pl.pallas_call(
        functools.partial(block_kernel, nneg),
        out_shape=(
            half,
            half,
            jax.ShapeDtypeStruct((PIECES, relrows, LANES), bf16),
            jax.ShapeDtypeStruct(r_rows.shape, f32),
        ),
        in_specs=[smem()] * 4 + [hbm()] * 3,
        out_specs=(hbm(), hbm(), hbm(), hbm()),
        scratch_shapes=[
            table, table, table, table, rel, rel,
            pltpu.VMEM((2, 512, dst_slab.shape[1]), bf16),
            pltpu.VMEM((2, FLAT, LANES), f32),
            pltpu.VMEM((2, FLAT, LANES), f32),
            pltpu.VMEM((HALF, LANES), f32),
            pltpu.VMEM((HALF, LANES), f32),
            pltpu.VMEM((HALF, LANES), f32),
            pltpu.VMEM((HALF, LANES), f32),
            pltpu.VMEM((SPAN, LANES * GROUPS), bf16),
            pltpu.VMEM((SPAN, LANES * GROUPS), bf16),
            pltpu.VMEM((SPAN, SPAN), bf16),
            pltpu.VMEM((SLOTS, packed, LANES), bf16),
            pltpu.VMEM((SLOTS, relrows, LANES), bf16),
            pltpu.SemaphoreType.DMA((2,)),
            pltpu.SemaphoreType.DMA((2, 2)),
            pltpu.SemaphoreType.DMA((2,)),
            pltpu.SemaphoreType.DMA((SLOTS,)),
        ],
        compiler_params=pltpu.CompilerParams(vmem_limit_bytes=VMEM),
        name="edge_blocks",
    )(count, rid, dst, neg, dst_slab, e_rows, r_rows)


def source_rows(count, src, values, rows):
    packed = rows // PIECES // 2 * 25 // 8
    half = jax.ShapeDtypeStruct((PIECES, packed, LANES), bf16)
    table = pltpu.VMEM((rows * GROUPS, LANES), f32)
    return pl.pallas_call(
        source_kernel,
        out_shape=(half, half),
        in_specs=[smem()] * 2 + [hbm()],
        out_specs=(hbm(), hbm()),
        scratch_shapes=[
            table, table, table, table,
            pltpu.VMEM((2, FLAT, LANES), f32),
            pltpu.VMEM((SLOTS, packed, LANES), bf16),
            pltpu.SemaphoreType.DMA((2,)),
            pltpu.SemaphoreType.DMA((SLOTS,)),
        ],
        compiler_params=pltpu.CompilerParams(vmem_limit_bytes=VMEM),
        cost_estimate=pl.CostEstimate(flops=0, bytes_accessed=60_000_000, transcendentals=0),
        name="source_rows",
    )(count, src, values)


def sum_kernel(rep, x_ref, after_ref, keep_ref, send_ref):
    n = keep_ref.shape[0]

    def total(r):
        at = pl.ds(pl.multiple_of(r * n, n), n)
        out = x_ref[0, at, :].astype(f32)
        for i in range(1, x_ref.shape[0]):
            out = out + x_ref[i, at, :].astype(f32)
        return out

    keep_ref[...] = total(rep[0])
    send_ref[...] = total(1 - rep[0]).astype(bf16)


def sum_sides(rep, x, after):
    n = x.shape[1] // 2
    return pl.pallas_call(
        sum_kernel,
        out_shape=(
            jax.ShapeDtypeStruct((n, LANES), f32),
            jax.ShapeDtypeStruct((n, LANES), bf16),
        ),
        in_specs=[smem(), pl.BlockSpec(memory_space=pltpu.VMEM), hbm()],
        compiler_params=pltpu.CompilerParams(vmem_limit_bytes=VMEM),
        name="sum_sides",
    )(rep, x, after)


def across(x, n):
    part = n // 8
    rest = x[3 * n : 3 * n + part].T
    rest = jnp.concatenate([rest[k * REST : (k + 1) * REST] for k in range(8)], axis=1)
    return jnp.concatenate([x[:n].T, x[n : 2 * n].T, x[2 * n : 3 * n].T, rest], axis=0)


def update_kernel(a_ref, b_ref, emb_ref, out_ref):
    width, n = emb_ref.shape
    g = a_ref[...] + b_ref[...].astype(f32)
    new = (emb_ref[...].astype(f32) - 0.5 * across(g, n)).astype(bf16)
    for i in range(n // LANES):
        out_ref[i * width : (i + 1) * width, :] = new[:, i * LANES : (i + 1) * LANES]


def update(a, b, emb):
    width, n = emb.shape
    return pl.pallas_call(
        update_kernel,
        out_shape=jax.ShapeDtypeStruct((width * n // LANES, LANES), bf16),
        compiler_params=pltpu.CompilerParams(vmem_limit_bytes=VMEM),
        name="update",
    )(a, b, emb)


def finish_kernel(place, a_ref, ar_ref, b0_ref, b1_ref, b2_ref, b3_ref, dirty_ref, up_ref, check_ref):
    width = up_ref.shape[0]
    half = dirty_ref.shape[1] // PIECES // 2
    blocks = [(a_ref, k, k, 0) for k in range(4)] + [(ar_ref, k, 4 + k, 0) for k in range(4)]
    for k, ref in enumerate((b0_ref, b1_ref, b2_ref, b3_ref)):
        blocks += [(ref, 0, k, half), (ref, 1, 4 + k, half)]
    for ref, i, at_place, off in blocks:
        start = pl.multiple_of(place[at_place] * 2 * half + off, half)
        for k in range(half // LANES):
            at = pl.ds(pl.multiple_of(start + k * LANES, LANES), LANES)
            x = ref[i, k * width : (k + 1) * width, :]
            up_ref[:, at] = x
            check_ref[:, at] = jnp.where(dirty_ref[:, at] == 1, x.astype(f32), 0.0).astype(bf16)


def finish(place, parts, dirty, width):
    out = jax.ShapeDtypeStruct((width, dirty.shape[1]), bf16)
    return pl.pallas_call(
        finish_kernel,
        in_specs=[smem()] + [pl.BlockSpec(memory_space=pltpu.VMEM)] * 7,
        out_shape=(out, out),
        compiler_params=pltpu.CompilerParams(vmem_limit_bytes=VMEM),
        name="finish",
    )(place, *parts, dirty)


def relation_kernel(m, order, x_ref, out_ref):
    cols = jnp.concatenate(
        [across(x_ref[order[i]].astype(f32), m) for i in range(PIECES)], axis=1
    )
    out_ref[...] = cols[:, : out_ref.shape[1]]


def relation_out(order, x, m, shape):
    return pl.pallas_call(
        functools.partial(relation_kernel, m),
        out_shape=jax.ShapeDtypeStruct(shape, f32),
        in_specs=[smem(), pl.BlockSpec(memory_space=pltpu.VMEM)],
        compiler_params=pltpu.CompilerParams(vmem_limit_bytes=VMEM),
        name="relation_out",
    )(order, x)


def by_side(x):
    sides = lax.axis_size("side")
    return lax.all_to_all(x.reshape(sides, -1, LANES), "side", 0, 0, tiled=True)


def around(x):
    return [x] + [shifted(x, "side", by) for by in (1, -1, 2)]


def both_reps(x):
    return [x, shifted(x, "rep", 1)]


def swapped(x, axis, bit):
    count = lax.axis_size(axis)
    return lax.ppermute(x, axis, [(i, i ^ bit) for i in range(count)])


def local(
    embeddings, relation, source_ids, relation_ids, target_ids, negative_ids, edge_counts, dirty
):
    rows, width = embeddings.shape
    nrel = relation.shape[0]
    doms = lax.axis_size("dom")
    count = edge_counts.reshape(1)
    nneg = negative_ids.shape[-1]
    src = source_ids.reshape(-1) * GROUPS
    rid = relation_ids.reshape(-1) * GROUPS
    dst = target_ids.reshape(-1) * GROUPS
    neg = (jnp.pad(negative_ids[0, 0, 0], ((0, 0), (0, SPAN - nneg))) * GROUPS).reshape(-1)
    me = lax.axis_index("side") * lax.axis_size("rep") + lax.axis_index("rep")
    piece = rows // PIECES
    half = piece // 2
    own = [lax.dynamic_slice_in_dim(embeddings.T, me * piece + h * half, half, 1) for h in (0, 1)]
    side, rep = lax.axis_index("side"), lax.axis_index("rep")
    sides = jnp.stack([side, (side + 3) % 4, (side + 1) % 4, (side + 2) % 4])
    place = jnp.concatenate([sides * 2 + rep, sides * 2 + 1 - rep]).astype(jnp.int32)
    order = jnp.argsort(place).astype(jnp.int32)

    dst_slab = shifted(embeddings, "dom", -1)
    e_rows, r_rows = edge_rows(count, src, rid, embeddings, relation)
    *gdst, grel, values = edge_blocks(nneg, count, rid, dst, neg, dst_slab, e_rows, r_rows, nrel)
    returned = [shifted(g, "dom", 1) for g in gdst]
    which = rep.reshape(1).astype(jnp.int32)
    rel = by_side(grel)
    gsrc = source_rows(count, src, values, rows)
    rel, sent = sum_sides(which, rel, gsrc[0])
    rel = (rel + shifted(sent, "rep", 1).astype(f32)).astype(bf16)
    bit = 1
    while bit < doms:
        rel = (rel.astype(f32) + swapped(rel, "dom", bit).astype(f32)).astype(bf16)
        bit *= 2
    rel = jnp.concatenate(around(jnp.stack(both_reps(rel))))
    relm = -(-nrel // (PIECES * 64)) * 64
    rel_order = (order % 4) * 2 + order // 4
    relation_grad = relation_out(rel_order, rel, relm, (width, nrel))

    mine = []
    for h in (0, 1):
        keep, sent = sum_sides(which, by_side(gsrc[h] + returned[h]), own[h])
        mine.append(update(keep, shifted(sent, "rep", 1), own[h]))
    a4 = jnp.stack(around(mine[0]))
    parts = both_reps(a4) + around(jnp.stack(both_reps(mine[1])))
    updated, checkpoint = finish(place, parts, dirty[None, :], width)
    return (updated.T, relation_grad.T, checkpoint.T)


def solution(mesh):
    placed = (
        P("dom", None),
        P(),
        P("dom", "side", "rep", None),
        P("dom", "side", "rep", None),
        P("dom", "side", "rep", None),
        P("dom", "side", "rep", None, None),
        P("dom", "side", "rep"),
        P("dom"),
    )
    return jax.shard_map(
        local,
        mesh=mesh,
        in_specs=placed,
        out_specs=(P("dom", None), P(), P("dom", None)),
        check_vma=False,
    )
```

```python
import functools

import jax
import jax.numpy as jnp
from jax import lax
from jax.experimental import pallas as pl
from jax.experimental.pallas import tpu as pltpu
from jax.sharding import PartitionSpec as P

SPAN = 1024
LANES = 128
GROUPS = 4
REST = 16
FLAT = SPAN * GROUPS
CHUNK = SPAN // 2
HALF = FLAT // 2
PIECES = 8
INE = 512
INN = 256
NCOPY = 3
SLOTS = 4
VMEM = 61 * 2**20

f32 = jnp.float32
bf16 = jnp.bfloat16


def shifted(x, axis, by):
    count = lax.axis_size(axis)
    return lax.ppermute(x, axis, [(i, (i + by) % count) for i in range(count)])


def row_of(index):
    return pl.ds(pl.multiple_of(index, GROUPS), GROUPS)


def slot_of(base, k):
    return pl.ds(base + (k // 8) * 8 * GROUPS + k % 8, GROUPS, stride=8)


def tiles(x):
    n = x.shape[0] // GROUPS
    x = x.reshape(n // 8, GROUPS, 8, LANES)
    return [x[:, c].reshape(n, LANES) for c in range(GROUPS)]


def untiles(cols):
    n = cols[0].shape[0]
    x = jnp.concatenate([c.reshape(n // 8, 1, 8, LANES) for c in cols], axis=1)
    return x.reshape(n * GROUPS, LANES)


def gather_rows(ops, base, n):
    for k0 in range(0, n, 8):
        ks = range(k0, k0 + 8)
        held = [[table[row_of(ids[j + k]), :] for table, ids, j, _ in ops] for k in ks]
        for k, rows in zip(ks, held):
            for (_, _, _, out), x in zip(ops, rows):
                out[slot_of(base, k), :] = x


def fill_rows(x, table, first, n):
    x = x.astype(f32)
    for c in range(GROUPS):
        part = x[:, c * LANES : min((c + 1) * LANES, x.shape[1])]
        if part.shape[1] < LANES:
            part = jnp.concatenate(
                [part, jnp.zeros((n, LANES - part.shape[1]), f32)], axis=1
            )
        table[pl.ds(first * GROUPS + c, n, stride=GROUPS), :] = part


def load_table(src_hbm, raw, sems, table):
    part = raw.shape[1]
    count = src_hbm.shape[0] // part

    def copy(i, slot):
        return pltpu.make_async_copy(
            src_hbm.at[pl.ds(pl.multiple_of(i * part, part), part)], raw.at[slot], sems.at[slot]
        )

    for i in range(2):
        copy(i, i).start()

    @pl.loop(0, count)
    def _(i):
        slot = lax.rem(i, 2)
        copy(i, slot).wait()

        @pl.loop(0, part // 64)
        def _(q):
            at = pl.multiple_of(q * 64, 64)
            fill_rows(raw[slot, pl.ds(at, 64), :], table, i * part + at, 64)

        @pl.when(i + 2 < count)
        def _():
            copy(i + 2, slot).start()


def edge_rows_kernel(
    count, src_i, rid_i, emb_hbm, rel_ref, e_out, r_out, ts, tr, raw, eb0, eb1, rb0, rb1, lsem, sems
):
    load_table(emb_hbm, raw, lsem, ts)
    nrel = rel_ref.shape[0]
    whole = nrel // 64

    @pl.loop(0, whole)
    def _(q):
        first = pl.multiple_of(q * 64, 64)
        fill_rows(rel_ref[pl.ds(first, 64), :], tr, first, 64)

    for i in range(whole * 64, nrel):
        fill_rows(rel_ref[i : i + 1, :], tr, i, 1)

    nblocks = (count[0] + SPAN - 1) // SPAN
    outs = ((eb0, e_out, 0), (eb1, e_out, 1), (rb0, r_out, 0), (rb1, r_out, 1))

    def copies(blk, slot):
        return [
            pltpu.make_async_copy(
                buf.at[slot], out.at[blk, pl.ds(h * HALF, HALF)], sems.at[slot, i]
            )
            for i, (buf, out, h) in enumerate(outs)
        ]

    def step(blk, _):
        slot = lax.rem(blk, 2)

        @pl.when(blk >= 2)
        def _():
            for c in copies(blk - 2, slot):
                c.wait()

        e0, e1, r0, r1 = (x.at[slot] for x in (eb0, eb1, rb0, rb1))

        @pl.loop(0, SPAN // 32)
        def _(q):
            base = pl.multiple_of(q * 16 * GROUPS, 64)
            j = blk * SPAN + q * 16
            gather_rows(
                [
                    (ts, src_i, j, e0),
                    (ts, src_i, j + SPAN // 2, e1),
                    (tr, rid_i, j, r0),
                    (tr, rid_i, j + SPAN // 2, r1),
                ],
                base,
                16,
            )

        for c in copies(blk, slot):
            c.start()
        return 0

    lax.fori_loop(0, nblocks, step, 0)

    @pl.when(nblocks >= 2)
    def _():
        for c in copies(nblocks - 2, lax.rem(nblocks, 2)):
            c.wait()

    for c in copies(nblocks - 1, lax.rem(nblocks + 1, 2)):
        c.wait()


def write_piece(first, n, load, stage):
    for c in range(GROUPS - 1):
        stage[c * n : (c + 1) * n, :] = load(c, first, n).astype(stage.dtype)
    part = n // 8
    rest = load(GROUPS - 1, first, part)
    for k in range(1, 8):
        rest = rest + pltpu.roll(load(GROUPS - 1, first + k * part, part), k * REST, 1)
    stage[3 * n : 3 * n + part, :] = rest.astype(stage.dtype)


def zero(acc):
    n = acc.shape[0]
    whole = n // 256

    @pl.loop(0, whole)
    def _(q):
        acc[pl.ds(pl.multiple_of(q * 256, 256), 256), :] = jnp.zeros((256, LANES), f32)

    if n % 256:
        acc[whole * 256 :, :] = jnp.zeros((n - whole * 256, LANES), f32)


def add_rows(ops):
    values = [val[at, :] for _, _, val, at in ops]
    held = [acc[row, :] for acc, row, _, _ in ops]
    for (acc, row, _, _), v, h in zip(ops, values, held):
        acc[row, :] = h + v


def plane(accs):
    def load(c, first, n):
        at = pl.ds(first * GROUPS + c, n, stride=GROUPS)
        x = accs[0][at, :]
        for acc in accs[1:]:
            x = x + acc[at, :]
        return x

    return load


def block_kernel(
    nneg, count, rid_i, dst_i, neg_i, dst_hbm, e_hbm, r_hbm,
    lo_out, hi_out, rel_out, v_out,
    td, a0, a1, a2, r0_acc, r1_acc, raw, eb, rb, db0, db1, nb0, nb1, lb, nbb, dn, stage, rstage, lsem, sems, vsem, osem,
):
    total = count[0]
    nblocks = (total + SPAN - 1) // SPAN

    def fetches(blk, slot):
        return (
            pltpu.make_async_copy(e_hbm.at[blk], eb.at[slot], sems.at[slot, 0]),
            pltpu.make_async_copy(r_hbm.at[blk], rb.at[slot], sems.at[slot, 1]),
        )

    def put(blk, slot):
        return pltpu.make_async_copy(rb.at[slot], v_out.at[blk], vsem.at[slot])

    for c in fetches(0, 0):
        c.start()
    load_table(dst_hbm, raw, lsem, td)
    for acc in (a0, a1, a2, r0_acc, r1_acc):
        zero(acc)

    def step(blk, _):
        slot = lax.rem(blk, 2)

        @pl.when(blk >= 1)
        def _():
            put(blk - 1, 1 - slot).wait()

        @pl.when(blk + 1 < nblocks)
        def _():
            for c in fetches(blk + 1, 1 - slot):
                c.start()

        first = blk * SPAN
        es, rs = eb.at[slot], rb.at[slot]

        @pl.loop(0, SPAN // 32)
        def _(q):
            base = pl.multiple_of(q * 16 * GROUPS, 64)
            j = first + q * 16
            gather_rows(
                [
                    (td, dst_i, j, db0),
                    (td, dst_i, j + CHUNK, db1),
                    (td, neg_i, j, nb0),
                    (td, neg_i, j + CHUNK, nb1),
                ],
                base,
                16,
            )

        for ch, nb in enumerate((nb0, nb1)):
            cols = tiles(nb[...])
            for c in range(GROUPS):
                nbb[ch * CHUNK : (ch + 1) * CHUNK, c * LANES : (c + 1) * LANES] = cols[c].astype(bf16)

        for c in fetches(blk, slot):
            c.wait()

        def dense(ch, db):
            r0 = ch * CHUNK
            flat = pl.ds(ch * HALF, HALF)
            e = tiles(es[flat, :])
            r = tiles(rs[flat, :])
            d = tiles(db[...])
            left = [(e[c] * r[c]).astype(bf16) for c in range(GROUPS)]
            leftf = [x.astype(f32) for x in left]
            prod = leftf[0] * d[0]
            for c in range(1, GROUPS):
                prod = prod + leftf[c] * d[c]
            positive = jnp.sum(prod, axis=1, keepdims=True)
            lc = jnp.concatenate(left, axis=1)
            lb[pl.ds(r0, CHUNK), :] = lc
            negative = lax.dot_general(
                lc, nbb[...], (((1,), (1,)), ((), ())), preferred_element_type=f32
            )
            edge = nneg // LANES * LANES
            lane = lax.broadcasted_iota(jnp.int32, (CHUNK, SPAN - edge), 1)
            negative = jnp.concatenate(
                [negative[:, :edge], jnp.where(lane < nneg - edge, negative[:, edge:], -jnp.inf)], axis=1
            )
            top = jnp.maximum(positive, jnp.max(negative, axis=1, keepdims=True))
            e_pos = jnp.exp(positive - top)
            e_neg = jnp.exp(negative - top)
            z = e_pos + jnp.sum(e_neg, axis=1, keepdims=True)
            row = lax.broadcasted_iota(jnp.int32, (CHUNK, 1), 0) + (first + r0)
            live = jnp.where(row < total, 1.0, 0.0).astype(f32)
            inv = 1.0 / z
            d_pos = live * (e_pos * inv - 1.0)
            d_neg = (e_neg * (live * inv)).astype(bf16)
            dn[pl.ds(r0, CHUNK), :] = d_neg
            dl = jnp.dot(d_neg, nbb[...], preferred_element_type=f32)
            x = [d_pos * d[c] + dl[:, c * LANES : (c + 1) * LANES] for c in range(GROUPS)]
            db[...] = untiles([d_pos * leftf[c] for c in range(GROUPS)])
            es[flat, :] = untiles([x[c] * e[c] for c in range(GROUPS)])
            rs[flat, :] = untiles([x[c] * r[c] for c in range(GROUPS)])


        def negative_rows(ch, nb):
            part = lax.dot_general(
                dn[:, ch * CHUNK : (ch + 1) * CHUNK], lb[...], (((0,), (0,)), ((), ())),
                preferred_element_type=f32,
            )
            nb[...] = untiles([part[:, c * LANES : (c + 1) * LANES] for c in range(GROUPS)])

        def add_edges(h, start, base, n):
            db, ev = (db0, db1)[h], es.at[pl.ds(h * HALF, HALF)]
            j0 = first + h * CHUNK + start
            for t in range(0, n, 2):
                ops = []
                for i in range(2):
                    k, at = t + i, slot_of(base, t + i)
                    ops.append(((a0, a1)[i], row_of(dst_i[j0 + k]), db, at))
                    ops.append(((r0_acc, r1_acc)[i], row_of(rid_i[j0 + k]), ev, at))
                add_rows(ops)

        def add_negatives(h, start, base, n):
            nb = (nb0, nb1)[h]
            j0 = first + h * CHUNK + start
            for t in range(0, n, NCOPY):
                add_rows(
                    [
                        ((a0, a1, a2)[i], row_of(neg_i[j0 + t + i]), nb, slot_of(base, t + i))
                        for i in range(min(NCOPY, n - t))
                    ]
                )

        def looped(step, h, start, stop):
            @pl.loop(0, (stop - start) // 32)
            def _(q):
                at = pl.multiple_of(start + q * 32, 32)
                step(h, at, pl.multiple_of(at * GROUPS, 128), 32)

        dense(0, db0)
        add_edges(0, 0, 0, CHUNK)
        dense(1, db1)
        put(blk, slot).start()
        add_edges(1, 0, 0, INE)
        negative_rows(0, nb0)
        add_negatives(0, 0, 0, INN)
        negative_rows(1, nb1)
        if INE < CHUNK:
            looped(add_edges, 1, INE, CHUNK)
        if INN < CHUNK:
            looped(add_negatives, 0, INN, CHUNK)
        looped(add_negatives, 1, 0, CHUNK)
        return 0

    lax.fori_loop(0, nblocks, step, 0)
    last = nblocks - 1
    put(last, lax.rem(last, 2)).wait()

    m = r0_acc.shape[0] // GROUPS // PIECES
    packed = m * 25 // 8
    grad, rel = plane((a0, a1, a2)), plane((r0_acc, r1_acc))

    def fill_rel(j, st):
        write_piece(j * m, m, rel, st)
        if st.shape[0] > packed:
            st[packed:, :] = jnp.zeros((st.shape[0] - packed, LANES), st.dtype)

    emit_halves(grad, td.shape[0] // GROUPS, lo_out, hi_out, stage, osem)
    emit(fill_rel, rel_out, rstage, osem)


def emit(fill, out, stage, sem):
    def copy(j, slot):
        return pltpu.make_async_copy(stage.at[slot], out.at[j], sem.at[slot])

    @pl.loop(0, PIECES)
    def _(j):
        slot = lax.rem(j, SLOTS)

        @pl.when(j >= SLOTS)
        def _():
            copy(j - SLOTS, slot).wait()

        fill(j, stage.at[slot])
        copy(j, slot).start()

    for j in range(PIECES - SLOTS, PIECES):
        copy(j, j % SLOTS).wait()


def emit_halves(load, rows, lo_out, hi_out, stage, sem):
    half = rows // PIECES // 2
    for h, out in enumerate((lo_out, hi_out)):
        emit(
            lambda j, st, h=h: write_piece((2 * j + h) * half, half, load, st), out, stage, sem
        )


def source_kernel(count, src_i, v_hbm, lo_out, hi_out, a0, a1, a2, a3, vb, stage, sems, osem):
    nblocks = (count[0] + SPAN - 1) // SPAN
    accs = (a0, a1, a2, a3)

    def fetch(blk, slot):
        return pltpu.make_async_copy(v_hbm.at[blk], vb.at[slot], sems.at[slot])

    fetch(0, 0).start()
    for acc in accs:
        zero(acc)

    def step(blk, _):
        slot = lax.rem(blk, 2)

        @pl.when(blk + 1 < nblocks)
        def _():
            fetch(blk + 1, 1 - slot).start()

        fetch(blk, slot).wait()
        vs = vb.at[slot]

        @pl.loop(0, SPAN // 32)
        def _(q):
            base = pl.multiple_of(q * 32 * GROUPS, 128)
            for t in range(0, 32, 4):
                add_rows(
                    [
                        (accs[i], row_of(src_i[blk * SPAN + q * 32 + t + i]), vs, slot_of(base, t + i))
                        for i in range(4)
                    ]
                )

        return 0

    lax.fori_loop(0, nblocks, step, 0)
    emit_halves(plane(accs), a0.shape[0] // GROUPS, lo_out, hi_out, stage, osem)


def smem():
    return pl.BlockSpec(memory_space=pltpu.SMEM)


def hbm():
    return pl.BlockSpec(memory_space=pl.ANY)


def edge_rows(count, src, rid, emb, relation):
    nb = src.shape[0] // SPAN
    rows = emb.shape[0]
    nrel = relation.shape[0]
    shape = jax.ShapeDtypeStruct((nb, FLAT, LANES), f32)
    return pl.pallas_call(
        edge_rows_kernel,
        out_shape=(shape, shape),
        in_specs=[smem()] * 3 + [hbm(), pl.BlockSpec(memory_space=pltpu.VMEM)],
        out_specs=(hbm(), hbm()),
        scratch_shapes=[
            pltpu.VMEM((rows * GROUPS, LANES), f32),
            pltpu.VMEM((-(-nrel // 8) * 8 * GROUPS, LANES), f32),
            pltpu.VMEM((2, 512, emb.shape[1]), bf16),
            pltpu.VMEM((2, HALF, LANES), f32),
            pltpu.VMEM((2, HALF, LANES), f32),
            pltpu.VMEM((2, HALF, LANES), f32),
            pltpu.VMEM((2, HALF, LANES), f32),
            pltpu.SemaphoreType.DMA((2,)),
            pltpu.SemaphoreType.DMA((2, 4)),
        ],
        compiler_params=pltpu.CompilerParams(vmem_limit_bytes=VMEM),
        cost_estimate=pl.CostEstimate(flops=0, bytes_accessed=60_000_000, transcendentals=0),
        name="edge_rows",
    )(count, src, rid, emb, relation)


def edge_blocks(nneg, count, rid, dst, neg, dst_slab, e_rows, r_rows, nrel):
    rows = dst_slab.shape[0]
    packed = rows // PIECES // 2 * 25 // 8
    half = jax.ShapeDtypeStruct((PIECES, packed, LANES), bf16)
    relm = -(-nrel // (PIECES * 64)) * 64
    relrows = -(-(relm * 25 // 8) // 128) * 128
    table = pltpu.VMEM((rows * GROUPS, LANES), f32)
    rel = pltpu.VMEM((relm * PIECES * GROUPS, LANES), f32)
    return pl.pallas_call(
        functools.partial(block_kernel, nneg),
        out_shape=(
            half,
            half,
            jax.ShapeDtypeStruct((PIECES, relrows, LANES), bf16),
            jax.ShapeDtypeStruct(r_rows.shape, f32),
        ),
        in_specs=[smem()] * 4 + [hbm()] * 3,
        out_specs=(hbm(), hbm(), hbm(), hbm()),
        scratch_shapes=[
            table, table, table, table, rel, rel,
            pltpu.VMEM((2, 512, dst_slab.shape[1]), bf16),
            pltpu.VMEM((2, FLAT, LANES), f32),
            pltpu.VMEM((2, FLAT, LANES), f32),
            pltpu.VMEM((HALF, LANES), f32),
            pltpu.VMEM((HALF, LANES), f32),
            pltpu.VMEM((HALF, LANES), f32),
            pltpu.VMEM((HALF, LANES), f32),
            pltpu.VMEM((SPAN, LANES * GROUPS), bf16),
            pltpu.VMEM((SPAN, LANES * GROUPS), bf16),
            pltpu.VMEM((SPAN, SPAN), bf16),
            pltpu.VMEM((SLOTS, packed, LANES), bf16),
            pltpu.VMEM((SLOTS, relrows, LANES), bf16),
            pltpu.SemaphoreType.DMA((2,)),
            pltpu.SemaphoreType.DMA((2, 2)),
            pltpu.SemaphoreType.DMA((2,)),
            pltpu.SemaphoreType.DMA((SLOTS,)),
        ],
        compiler_params=pltpu.CompilerParams(vmem_limit_bytes=VMEM),
        name="edge_blocks",
    )(count, rid, dst, neg, dst_slab, e_rows, r_rows)


def source_rows(count, src, values, rows):
    packed = rows // PIECES // 2 * 25 // 8
    half = jax.ShapeDtypeStruct((PIECES, packed, LANES), bf16)
    table = pltpu.VMEM((rows * GROUPS, LANES), f32)
    return pl.pallas_call(
        source_kernel,
        out_shape=(half, half),
        in_specs=[smem()] * 2 + [hbm()],
        out_specs=(hbm(), hbm()),
        scratch_shapes=[
            table, table, table, table,
            pltpu.VMEM((2, FLAT, LANES), f32),
            pltpu.VMEM((SLOTS, packed, LANES), bf16),
            pltpu.SemaphoreType.DMA((2,)),
            pltpu.SemaphoreType.DMA((SLOTS,)),
        ],
        compiler_params=pltpu.CompilerParams(vmem_limit_bytes=VMEM),
        cost_estimate=pl.CostEstimate(flops=0, bytes_accessed=60_000_000, transcendentals=0),
        name="source_rows",
    )(count, src, values)


def sum_kernel(rep, x_ref, after_ref, keep_ref, send_ref):
    n = keep_ref.shape[0]

    def total(r):
        at = pl.ds(pl.multiple_of(r * n, n), n)
        out = x_ref[0, at, :].astype(f32)
        for i in range(1, x_ref.shape[0]):
            out = out + x_ref[i, at, :].astype(f32)
        return out

    keep_ref[...] = total(rep[0])
    send_ref[...] = total(1 - rep[0]).astype(bf16)


def sum_sides(rep, x, after):
    n = x.shape[1] // 2
    return pl.pallas_call(
        sum_kernel,
        out_shape=(
            jax.ShapeDtypeStruct((n, LANES), f32),
            jax.ShapeDtypeStruct((n, LANES), bf16),
        ),
        in_specs=[smem(), pl.BlockSpec(memory_space=pltpu.VMEM), hbm()],
        compiler_params=pltpu.CompilerParams(vmem_limit_bytes=VMEM),
        name="sum_sides",
    )(rep, x, after)


def across(x, n):
    part = n // 8
    rest = x[3 * n : 3 * n + part].T
    rest = jnp.concatenate([rest[k * REST : (k + 1) * REST] for k in range(8)], axis=1)
    return jnp.concatenate([x[:n].T, x[n : 2 * n].T, x[2 * n : 3 * n].T, rest], axis=0)


def update_kernel(a_ref, b_ref, emb_ref, out_ref):
    width, n = emb_ref.shape
    g = a_ref[...] + b_ref[...].astype(f32)
    new = (emb_ref[...].astype(f32) - 0.5 * across(g, n)).astype(bf16)
    for i in range(n // LANES):
        out_ref[i * width : (i + 1) * width, :] = new[:, i * LANES : (i + 1) * LANES]


def update(a, b, emb):
    width, n = emb.shape
    return pl.pallas_call(
        update_kernel,
        out_shape=jax.ShapeDtypeStruct((width * n // LANES, LANES), bf16),
        compiler_params=pltpu.CompilerParams(vmem_limit_bytes=VMEM),
        name="update",
    )(a, b, emb)


def finish_kernel(place, a_ref, ar_ref, b0_ref, b1_ref, b2_ref, b3_ref, dirty_ref, up_ref, check_ref):
    width = up_ref.shape[0]
    half = dirty_ref.shape[1] // PIECES // 2
    blocks = [(a_ref, k, k, 0) for k in range(4)] + [(ar_ref, k, 4 + k, 0) for k in range(4)]
    for k, ref in enumerate((b0_ref, b1_ref, b2_ref, b3_ref)):
        blocks += [(ref, 0, k, half), (ref, 1, 4 + k, half)]
    for ref, i, at_place, off in blocks:
        start = pl.multiple_of(place[at_place] * 2 * half + off, half)
        for k in range(half // LANES):
            at = pl.ds(pl.multiple_of(start + k * LANES, LANES), LANES)
            x = ref[i, k * width : (k + 1) * width, :]
            up_ref[:, at] = x
            check_ref[:, at] = jnp.where(dirty_ref[:, at] == 1, x.astype(f32), 0.0).astype(bf16)


def finish(place, parts, dirty, width):
    out = jax.ShapeDtypeStruct((width, dirty.shape[1]), bf16)
    return pl.pallas_call(
        finish_kernel,
        in_specs=[smem()] + [pl.BlockSpec(memory_space=pltpu.VMEM)] * 7,
        out_shape=(out, out),
        compiler_params=pltpu.CompilerParams(vmem_limit_bytes=VMEM),
        name="finish",
    )(place, *parts, dirty)


def relation_kernel(m, order, x_ref, out_ref):
    cols = jnp.concatenate(
        [across(x_ref[order[i]].astype(f32), m) for i in range(PIECES)], axis=1
    )
    out_ref[...] = cols[:, : out_ref.shape[1]]


def relation_out(order, x, m, shape):
    return pl.pallas_call(
        functools.partial(relation_kernel, m),
        out_shape=jax.ShapeDtypeStruct(shape, f32),
        in_specs=[smem(), pl.BlockSpec(memory_space=pltpu.VMEM)],
        compiler_params=pltpu.CompilerParams(vmem_limit_bytes=VMEM),
        name="relation_out",
    )(order, x)


def by_side(x):
    sides = lax.axis_size("side")
    return lax.all_to_all(x.reshape(sides, -1, LANES), "side", 0, 0, tiled=True)


def around(x):
    return [x] + [shifted(x, "side", by) for by in (1, -1, 2)]


def both_reps(x):
    return [x, shifted(x, "rep", 1)]


def swapped(x, axis, bit):
    count = lax.axis_size(axis)
    return lax.ppermute(x, axis, [(i, i ^ bit) for i in range(count)])


def local(
    embeddings, relation, source_ids, relation_ids, target_ids, negative_ids, edge_counts, dirty
):
    rows, width = embeddings.shape
    nrel = relation.shape[0]
    doms = lax.axis_size("dom")
    count = edge_counts.reshape(1)
    nneg = negative_ids.shape[-1]
    src = source_ids.reshape(-1) * GROUPS
    rid = relation_ids.reshape(-1) * GROUPS
    dst = target_ids.reshape(-1) * GROUPS
    neg = (jnp.pad(negative_ids[0, 0, 0], ((0, 0), (0, SPAN - nneg))) * GROUPS).reshape(-1)
    me = lax.axis_index("side") * lax.axis_size("rep") + lax.axis_index("rep")
    piece = rows // PIECES
    half = piece // 2
    own = [lax.dynamic_slice_in_dim(embeddings.T, me * piece + h * half, half, 1) for h in (0, 1)]
    side, rep = lax.axis_index("side"), lax.axis_index("rep")
    sides = jnp.stack([side, (side + 3) % 4, (side + 1) % 4, (side + 2) % 4])
    place = jnp.concatenate([sides * 2 + rep, sides * 2 + 1 - rep]).astype(jnp.int32)
    order = jnp.argsort(place).astype(jnp.int32)

    dst_slab = shifted(embeddings, "dom", -1)
    e_rows, r_rows = edge_rows(count, src, rid, embeddings, relation)
    *gdst, grel, values = edge_blocks(nneg, count, rid, dst, neg, dst_slab, e_rows, r_rows, nrel)
    returned = [shifted(g, "dom", 1) for g in gdst]
    which = rep.reshape(1).astype(jnp.int32)
    rel = by_side(grel)
    gsrc = source_rows(count, src, values, rows)
    rel, sent = sum_sides(which, rel, gsrc[0])
    rel = (rel + shifted(sent, "rep", 1).astype(f32)).astype(bf16)
    bit = 1
    while bit < doms:
        rel = (rel.astype(f32) + swapped(rel, "dom", bit).astype(f32)).astype(bf16)
        bit *= 2
    rel = jnp.concatenate(around(jnp.stack(both_reps(rel))))
    relm = -(-nrel // (PIECES * 64)) * 64
    rel_order = (order % 4) * 2 + order // 4
    relation_grad = relation_out(rel_order, rel, relm, (width, nrel))

    mine = []
    for h in (0, 1):
        keep, sent = sum_sides(which, by_side(gsrc[h] + returned[h]), own[h])
        mine.append(update(keep, shifted(sent, "rep", 1), own[h]))
    a4 = jnp.stack(around(mine[0]))
    parts = both_reps(a4) + around(jnp.stack(both_reps(mine[1])))
    updated, checkpoint = finish(place, parts, dirty[None, :], width)
    return (updated.T, relation_grad.T, checkpoint.T)


def solution(mesh):
    placed = (
        P("dom", None),
        P(),
        P("dom", "side", "rep", None),
        P("dom", "side", "rep", None),
        P("dom", "side", "rep", None),
        P("dom", "side", "rep", None, None),
        P("dom", "side", "rep"),
        P("dom"),
    )
    return jax.shard_map(
        local,
        mesh=mesh,
        in_specs=placed,
        out_specs=(P("dom", None), P(), P("dom", None)),
        check_vma=False,
    )
```
